32 devices in a mesh: groups: 2 (over y), wide: 4 (over z), narrow: 2 (over x), pair: 2 (over core).
Axes of the slice: x: 2, y: 2, z: 4, core: 2. Of those that a mesh axis runs over, the one named last changes fastest.
Arguments:
- volume: bfloat16 [48, 16, 64, 128], P(('groups', 'wide'), 'narrow', 'pair'), parts along dimension 0, may hold values from -6 to 6
- w_encode: bfloat16 [3, 3, 3, 128, 128], replicated, may hold values from -0.109375 to 0.109375
- b_encode: float32 [128], replicated, may hold values from -3 to 3
- w_down: bfloat16 [2, 2, 2, 128, 256], replicated, may hold values from -0.1875 to 0.1875
- b_down: float32 [256], replicated, may hold values from -3 to 3
- w_bottom: bfloat16 [3, 3, 3, 256, 256], replicated, may hold values from -0.078125 to 0.078125
- b_bottom: float32 [256], replicated, may hold values from -3 to 3
- w_up: bfloat16 [2, 2, 2, 256, 128], replicated, may hold values from -0.375 to 0.375
- b_up: float32 [128], replicated, may hold values from -3 to 3
- w_decode: bfloat16 [3, 3, 3, 256, 128], replicated, may hold values from -0.078125 to 0.078125
- b_decode: float32 [128], replicated, may hold values from -3 to 3
Outputs:
- decoded: bfloat16 [48, 16, 64, 128], P(('groups', 'wide'), 'narrow', 'pair'), parts along dimension 0
The draws below stay inside these ranges and needn't reach their ends.
There are 2 independent parts, one for each index of `groups`. The reference program is written for one: setup_inputs(seed, part) draws one part's arguments, and reference() takes and returns one part's arrays. A program takes and returns all parts, laid end to end along the dimension named above; an argument that names none is the same for every part. Nothing has to cross between parts.
All inputs are finite; a program needn't handle non-finite values.
Results may differ from the reference program's by a relative error of at most 0.008.
Values may be sent and summed in bfloat16 or wider, within the bound.
A program may use at most 64 MiB of HBM per device.

```python
import jax
import jax.numpy as jnp
from jax import lax

C2 = 128
C3 = 256
DEPTH = 24
HEIGHT = 16
WIDTH = 64


def shard_levels(stream_key, extent, shards, least, high):
    loudness = 1.0
    for dim, shards_of in shards:
        heights = jax.random.uniform(jax.random.fold_in(jax.random.fold_in(stream_key, 6), dim), (shards_of,), jnp.float32, least / len(shards), high / len(shards))
        loudness = loudness * jnp.repeat(jnp.exp(heights), extent[dim] // shards_of).reshape((-1,) + (1,) * (len(extent) - 1 - dim))
    return loudness


def gaussian(own_key, dims, scale, bound, split=(), dtype=jnp.bfloat16):
    result = scale * jax.random.normal(own_key, dims, jnp.float32)
    if split:
        result = result * shard_levels(own_key, dims, split, -0.22, 0.18)
    return jnp.clip(result, -bound, bound).astype(dtype)


def setup_inputs(seed: int = 0, part: int = 0) -> dict:
    arg_keys = jax.random.split(jax.random.key(seed), 12)
    own_keys = jax.random.split(jax.random.fold_in(arg_keys[11], part), 12)
    return {
        "volume": gaussian(own_keys[0], (DEPTH, HEIGHT, WIDTH, C2), 1.0, 6.0, ((0, 4), (1, 2), (2, 2))),
        "w_encode": gaussian(arg_keys[1], (3, 3, 3, C2, C2), (27 * C2) ** -0.5, 0.109375),
        "b_encode": gaussian(arg_keys[2], (C2,), 0.5, 3.0, (), jnp.float32),
        "w_down": gaussian(arg_keys[3], (2, 2, 2, C2, C3), (8 * C2) ** -0.5, 0.1875),
        "b_down": gaussian(arg_keys[4], (C3,), 0.5, 3.0, (), jnp.float32),
        "w_bottom": gaussian(arg_keys[5], (3, 3, 3, C3, C3), (27 * C3) ** -0.5, 0.078125),
        "b_bottom": gaussian(arg_keys[6], (C3,), 0.5, 3.0, (), jnp.float32),
        "w_up": gaussian(arg_keys[7], (2, 2, 2, C3, C2), C3 ** -0.5, 0.375),
        "b_up": gaussian(arg_keys[8], (C2,), 0.5, 3.0, (), jnp.float32),
        "w_decode": gaussian(arg_keys[9], (3, 3, 3, 2 * C2, C2), (54 * C2) ** -0.5, 0.078125),
        "b_decode": gaussian(arg_keys[10], (C2,), 0.5, 3.0, (), jnp.float32),
    }


def leaky_relu(values):
    return jnp.maximum(values, 0.01 * values)


def conv_cube(field, kernel):
    return lax.conv_general_dilated(
        field.astype(jnp.float32)[None], kernel.astype(jnp.float32), (1, 1, 1),
        ((1, 1), (1, 1), (1, 1)), dimension_numbers=("NDHWC", "DHWIO", "NDHWC"),
        precision=lax.Precision.HIGHEST)[0]


def reference(volume, w_encode, b_encode, w_down, b_down, w_bottom, b_bottom, w_up, b_up, w_decode, b_decode):
    encoded = leaky_relu(conv_cube(volume, w_encode) + b_encode).astype(jnp.bfloat16)
    depth_cells, height_cells, width_cells, skip_width = encoded.shape
    blocks = encoded.astype(jnp.float32).reshape(depth_cells // 2, 2, height_cells // 2, 2, width_cells // 2, 2, skip_width)
    coarse = leaky_relu(jnp.einsum("zaybxci,abcio->zyxo", blocks, w_down.astype(jnp.float32),
                                   precision=lax.Precision.HIGHEST) + b_down).astype(jnp.bfloat16)
    bottom = leaky_relu(conv_cube(coarse, w_bottom) + b_bottom).astype(jnp.bfloat16)
    lifted = jnp.einsum("zyxi,abcio->zaybxco", bottom.astype(jnp.float32), w_up.astype(jnp.float32),
                        precision=lax.Precision.HIGHEST) + b_up
    raised = lifted.reshape(depth_cells, height_cells, width_cells, skip_width).astype(jnp.bfloat16)
    joined = jnp.concatenate([raised, encoded], axis=-1)
    return leaky_relu(conv_cube(joined, w_decode) + b_decode).astype(jnp.bfloat16)
```

```python
import functools
import itertools

import jax
import jax.numpy as jnp
from jax import lax
from jax.experimental import pallas as pl
from jax.experimental.pallas import tpu as pltpu
from jax.sharding import PartitionSpec as P

leak_slope = 0.01
MESH = pl.DeviceIdType.MESH
lead = 8
plane_steps = [s for s in itertools.product((-1, 0, 1), repeat=2) if s != (0, 0)]
width_steps = (-1, 1)


def leaky_relu(values):
    return jnp.maximum(values, leak_slope * values)


def rounded(values):
    return values.astype(jnp.bfloat16)


def source_span(step, cells, base):
    if step == 0:
        return pl.ds(base, cells)
    return pl.ds(base + (0 if step < 0 else cells - 1), 1)


def target_span(step, cells):
    if step == 0:
        return pl.ds(1, cells)
    return pl.ds(cells + 1 if step < 0 else 0, 1)


def kernel(
    sizes,
    volume,
    w_encode,
    w_down,
    w_bottom,
    w_up,
    w_decode,
    b_encode_far,
    b_down_far,
    b_bottom_far,
    b_up_far,
    b_decode_far,
    decoded,
    v_cells,
    e_cells,
    r_cells,
    c_cells,
    v_frame,
    e_frame,
    r_frame,
    c_frame,
    v_taps,
    e_taps,
    r_taps,
    c_taps,
    edge_out,
    edge_in,
    c_edge_out,
    c_edge_in,
    encode_pairs,
    skip_pairs,
    raised_pairs,
    down_matrix,
    bottom_matrix,
    up_matrix,
    down_rows,
    partial,
    result,
    b_encode,
    b_down,
    b_bottom,
    b_up,
    b_decode,
    send_sem,
    recv_sem,
    edge_send_sem,
    edge_recv_sem,
    load_sem,
    store_sem,
):
    depth, height, width, skip = volume.shape
    half_depth, half_height, half_width = depth // 2, height // 2, width // 2
    deep = w_down.shape[-1]
    deep_size, high_size, wide_size = sizes
    at_deep, at_high, at_wide = (lax.axis_index(name) for name in ("wide", "narrow", "pair"))

    def inside(place, step, size):
        return jnp.logical_and(place + step >= 0, place + step < size)

    def plane_exists(step):
        return jnp.logical_and(
            inside(at_deep, step[0], deep_size), inside(at_high, step[1], high_size)
        )

    def width_exists(step):
        return inside(at_wide, step, wide_size)

    plane_used = [
        s
        for s in plane_steps
        if (s[0] == 0 or deep_size > 1) and (s[1] == 0 or high_size > 1)
    ]
    width_used = width_steps if wide_size > 1 else ()

    loads = []

    def load(source, target):
        copy = pltpu.make_async_copy(source, target, load_sem.at[len(loads)])
        copy.start()
        loads.append(copy)
        return copy

    own_load = load(volume, v_cells.at[pl.ds(1, depth), pl.ds(1, height)])

    def load_pairs(weight, first, target):
        return [
            load(
                weight.at[a, :, :, pl.ds(first, skip), :],
                target.at[a, pl.ds(j, 3), :, :, pl.ds(j * skip, skip)],
            )
            for a in range(3)
            for j in range(2)
        ]

    encode_loads = load_pairs(w_encode, 0, encode_pairs)
    encode_loads += [
        load(b_encode_far, b_encode),
        load(b_down_far, b_down),
        load(b_bottom_far, b_bottom),
        load(b_up_far, b_up),
        load(b_decode_far, b_decode),
    ]
    down_load = load(w_down, down_matrix)

    def zero_halo(cells, planes, rows):
        blank = jnp.zeros(cells.shape[2:], cells.dtype)
        for z in range(planes + 2):
            for y in range(rows + 2):
                if z in (0, planes + 1) or y in (0, rows + 1):
                    cells[z, y] = blank

    for cells in (v_cells, e_cells, r_cells):
        zero_halo(cells, depth, height)
    zero_halo(c_cells, half_depth, half_height)
    edge_in[...] = jnp.zeros_like(edge_in)
    c_edge_in[...] = jnp.zeros_like(c_edge_in)

    barrier = pltpu.get_barrier_semaphore()
    for step in plane_used:

        @pl.when(plane_exists(step))
        def _():
            pl.semaphore_signal(
                barrier,
                inc=1,
                device_id={"wide": at_deep + step[0], "narrow": at_high + step[1]},
                device_id_type=MESH,
            )

    for step in width_used:

        @pl.when(width_exists(step))
        def _():
            pl.semaphore_signal(
                barrier, inc=1, device_id={"pair": at_wide + step}, device_id_type=MESH
            )

    peers = sum(
        [plane_exists(step).astype(jnp.int32) for step in plane_used]
        + [width_exists(step).astype(jnp.int32) for step in width_used]
    )
    pl.semaphore_wait(barrier, peers)

    started = []

    def send_planes(slot, cells, source, base, planes, rows):
        copies = []
        for k, step in enumerate(plane_used):
            copy = pltpu.make_async_remote_copy(
                src_ref=source.at[
                    source_span(step[0], planes, base), source_span(step[1], rows, base)
                ],
                dst_ref=cells.at[target_span(step[0], planes), target_span(step[1], rows)],
                send_sem=send_sem.at[slot, k],
                recv_sem=recv_sem.at[slot, k],
                device_id={"wide": at_deep + step[0], "narrow": at_high + step[1]},
                device_id_type=MESH,
            )
            pl.when(plane_exists(step))(copy.start)
            copies.append((plane_exists((-step[0], -step[1])), copy))
            started.append((plane_exists(step), copy))
        return copies

    def send_edges(slot, out, arriving):
        copies = []
        for k, step in enumerate(width_used):
            copy = pltpu.make_async_remote_copy(
                src_ref=out.at[k],
                dst_ref=arriving.at[k],
                send_sem=edge_send_sem.at[slot, k],
                recv_sem=edge_recv_sem.at[slot, k],
                device_id={"pair": at_wide + step},
                device_id_type=MESH,
            )
            pl.when(width_exists(step))(copy.start)
            copies.append((width_exists(-step), copy))
            started.append((width_exists(step), copy))
        return copies

    def arrive(copies):
        for exists, copy in copies:
            pl.when(exists)(copy.wait_recv)

    def take_edges(frame, out, cells):
        count, pitch, channels = frame.shape
        flat = frame.reshape(count * pitch, channels)
        out[0] = rounded(flat[pl.ds(lead, count, stride=pitch), :])
        out[1] = rounded(flat[pl.ds(lead + cells - 1, count, stride=pitch), :])

    def lanes(h):
        return pl.ds(h * skip, skip)

    def put_edges(frame, arriving, cells):
        count, pitch, channels = frame.shape
        flat = frame.reshape(count * pitch, channels)
        flat[pl.ds(lead + cells, count, stride=pitch), :] = arriving[0].astype(jnp.float32)
        flat[pl.ds(lead - 1, count, stride=pitch), :] = arriving[1].astype(jnp.float32)

    def halo_to_frame(cells, frame, planes, rows, span):
        for z in range(planes + 2):
            for y in range(rows + 2):
                if z in (0, planes + 1) or y in (0, rows + 1):
                    frame[z * (rows + 2) + y, lead : lead + span, :] = cells[z, y].astype(
                        jnp.float32
                    )

    deep_parts = range(deep // skip)

    def spread_taps(frame, taps):
        def one(z, carry):
            for y in range(height + 2):
                for c in range(3):
                    taps[z, y // 2, y % 2, :, c * skip : (c + 1) * skip] = rounded(
                        frame[z * (height + 2) + y, lead - 1 + c : lead - 1 + c + width, :]
                    )
            return carry

        lax.fori_loop(0, depth + 2, one, 0)

    def pair_conv(taps, matrix, z):
        total = None
        for a in range(3):
            rows = jnp.concatenate(
                [
                    taps[pl.ds(z + a, 2), pl.ds(r // 2, half_height), r % 2].reshape(
                        2 * half_height * width, 3 * skip
                    )
                    for r in range(4)
                ],
                axis=-1,
            )
            term = jnp.dot(
                rows,
                matrix[a].reshape(12 * skip, 2 * skip),
                preferred_element_type=jnp.float32,
            )
            total = term if total is None else total + term
        return total

    v_copies = send_planes(0, v_cells, volume, 0, depth, height)
    bottom_load = load(w_bottom, bottom_matrix)
    skip_loads = load_pairs(w_decode, skip, skip_pairs)
    up_loads = [
        load(
            w_up.at[a, b, c],
            up_matrix.at[:, pl.ds(((a * 2 + b) * 2 + c) * skip, skip)],
        )
        for a, b, c in itertools.product((0, 1), repeat=3)
    ]
    raised_loads = load_pairs(w_decode, 0, raised_pairs)
    for pairs in (encode_pairs, skip_pairs, raised_pairs):
        for a in range(3):
            pairs[a, 0, :, :, skip : 2 * skip] = jnp.zeros((3, skip, skip), jnp.bfloat16)
            pairs[a, 3, :, :, 0:skip] = jnp.zeros((3, skip, skip), jnp.bfloat16)
    c_frame[...] = jnp.zeros_like(c_frame)
    own_load.wait()
    arrive(v_copies)

    def widen(z, carry):
        for y in range(height + 2):
            v_frame[z * (height + 2) + y, lead : lead + width, :] = v_cells[z, y].astype(
                jnp.float32
            )
        return carry

    lax.fori_loop(0, depth + 2, widen, 0)
    take_edges(v_frame, edge_out.at[0], width)
    v_edges = send_edges(0, edge_out.at[0], edge_in.at[0])
    for copy in encode_loads:
        copy.wait()
    arrive(v_edges)
    put_edges(v_frame, edge_in.at[0], width)
    spread_taps(v_frame, v_taps)
    encode_bias = jnp.concatenate([b_encode[...], b_encode[...]], axis=-1)

    def encode(i, carry):
        z = 2 * i
        values = rounded(leaky_relu(pair_conv(v_taps, encode_pairs, z) + encode_bias))
        values = values.reshape(2, half_height, width, 2 * skip)
        for dz in range(2):
            for y in range(height):
                cells = values[dz, y // 2, :, (y % 2) * skip : (y % 2 + 1) * skip]
                e_cells[z + dz + 1, y + 1] = cells
                e_frame[
                    (z + dz + 1) * (height + 2) + y + 1, lead : lead + width, :
                ] = cells.astype(jnp.float32)
        return carry

    lax.fori_loop(0, half_depth, encode, 0)
    e_copies = send_planes(1, e_cells, e_cells, 1, depth, height)

    def gather_down(z, carry):
        for y in range(half_height):
            for a, b, c in itertools.product((0, 1), repeat=3):
                tap = (a * 2 + b) * 2 + c
                down_rows[z, y, :, tap * skip : (tap + 1) * skip] = rounded(
                    e_frame[
                        (2 * z + a + 1) * (height + 2) + 2 * y + b + 1,
                        pl.ds(lead + c, half_width, stride=2),
                        :,
                    ]
                )
        return carry

    lax.fori_loop(0, half_depth, gather_down, 0)
    down_load.wait()
    low_cells = half_depth * half_height * half_width
    coarse = jnp.dot(
        down_rows[...].reshape(low_cells, 8 * skip),
        down_matrix[...].reshape(8 * skip, deep),
        preferred_element_type=jnp.float32,
    )
    coarse = rounded(leaky_relu(coarse + b_down[...]))
    coarse = coarse.reshape(half_depth, half_height, half_width, deep)
    c_cells[1 : 1 + half_depth, 1 : 1 + half_height] = coarse
    c_copies = send_planes(2, c_cells, c_cells, 1, half_depth, half_height)
    for z in range(half_depth):
        for y in range(half_height):
            for h in deep_parts:
                c_frame[
                    h, (z + 1) * (half_height + 2) + y + 1, lead : lead + half_width, :
                ] = coarse[z, y, :, h * skip : (h + 1) * skip].astype(jnp.float32)

    arrive(e_copies)
    halo_to_frame(e_cells, e_frame, depth, height, width)
    take_edges(e_frame, edge_out.at[1], width)
    e_edges = send_edges(1, edge_out.at[1], edge_in.at[1])

    arrive(c_copies)
    for h in deep_parts:
        part = c_cells.at[:, :, :, lanes(h)]
        halo_to_frame(part, c_frame.at[h], half_depth, half_height, half_width)
        take_edges(c_frame.at[h], c_edge_out.at[:, :, lanes(h)], half_width)
    c_edges = send_edges(2, c_edge_out, c_edge_in)

    arrive(e_edges)
    put_edges(e_frame, edge_in.at[1], width)
    spread_taps(e_frame, e_taps)
    for copy in skip_loads:
        copy.wait()

    def decode_skip(i):
        partial[i] = pair_conv(e_taps, skip_pairs, 2 * i)

    decode_skip(0)

    arrive(c_edges)
    for h in deep_parts:
        put_edges(c_frame.at[h], c_edge_in.at[:, :, lanes(h)], half_width)
    for z in range(half_depth + 2):
        for y in range(half_height + 2):
            for c, h in itertools.product(range(3), deep_parts):
                first = c * deep + h * skip
                c_taps[z, y, :, first : first + skip] = rounded(
                    c_frame[
                        h, z * (half_height + 2) + y, lead - 1 + c : lead - 1 + c + half_width, :
                    ]
                )
    bottom_load.wait()
    total = jnp.zeros((low_cells, deep), jnp.float32)
    for a in range(3):
        for b in range(3):
            total += jnp.dot(
                c_taps[a : a + half_depth, b : b + half_height].reshape(low_cells, 3 * deep),
                bottom_matrix[a, b].reshape(3 * deep, deep),
                preferred_element_type=jnp.float32,
            )
    bottom = rounded(leaky_relu(total + b_bottom[...]))
    for copy in up_loads:
        copy.wait()
    up_bias = jnp.concatenate([b_up[...], b_up[...]], axis=-1)
    for a in range(2):
        for b in range(2):
            first = (a * 2 + b) * 2 * skip
            lifted = jnp.dot(
                bottom, up_matrix[:, first : first + 2 * skip], preferred_element_type=jnp.float32
            )
            lifted = rounded(lifted + up_bias).astype(jnp.float32)
            lifted = lifted.reshape(half_depth, half_height, half_width, 2 * skip)
            for z in range(half_depth):
                for y in range(half_height):
                    plane = (2 * z + a + 1) * (height + 2) + 2 * y + b + 1
                    for c in range(2):
                        r_frame[plane, pl.ds(lead + c, half_width, stride=2), :] = lifted[
                            z, y, :, c * skip : (c + 1) * skip
                        ]

    def narrow_raised(z, carry):
        for y in range(height):
            r_cells[z + 1, y + 1] = rounded(
                r_frame[(z + 1) * (height + 2) + y + 1, lead : lead + width, :]
            )
        return carry

    lax.fori_loop(0, depth, narrow_raised, 0)
    r_copies = send_planes(3, r_cells, r_cells, 1, depth, height)

    chunks = list(range(1, half_depth))
    for i in chunks[: len(chunks) // 2]:
        decode_skip(i)
    arrive(r_copies)
    halo_to_frame(r_cells, r_frame, depth, height, width)
    take_edges(r_frame, edge_out.at[2], width)
    r_edges = send_edges(3, edge_out.at[2], edge_in.at[2])
    for i in chunks[len(chunks) // 2 :]:
        decode_skip(i)
    arrive(r_edges)
    put_edges(r_frame, edge_in.at[2], width)
    spread_taps(r_frame, r_taps)
    for copy in raised_loads:
        copy.wait()
    decode_bias = jnp.concatenate([b_decode[...], b_decode[...]], axis=-1)
    stores = []
    for i in range(half_depth):
        values = pair_conv(r_taps, raised_pairs, 2 * i) + partial[i]
        values = rounded(leaky_relu(values + decode_bias))
        values = values.reshape(2, half_height, width, 2 * skip)
        for dz in range(2):
            for y in range(height):
                result[2 * i + dz, y] = values[
                    dz, y // 2, :, (y % 2) * skip : (y % 2 + 1) * skip
                ]
        store = pltpu.make_async_copy(
            result.at[pl.ds(2 * i, 2)], decoded.at[pl.ds(2 * i, 2)], store_sem.at[i]
        )
        store.start()
        stores.append(store)
    for exists, copy in started:
        pl.when(exists)(copy.wait_send)
    for store in stores:
        store.wait()


def body(
    sizes,
    volume,
    w_encode,
    b_encode,
    w_down,
    b_down,
    w_bottom,
    b_bottom,
    w_up,
    b_up,
    w_decode,
    b_decode,
):
    depth, height, width, skip = volume.shape
    deep = w_down.shape[-1]
    half_depth, half_height, half_width = depth // 2, height // 2, width // 2
    planes = (depth + 2) * (height + 2)
    planes += -planes % 16
    low_planes = (half_depth + 2) * (half_height + 2)
    low_planes += -low_planes % 16
    half = jnp.bfloat16
    cells = pltpu.VMEM((depth + 2, height + 2, width, skip), half)
    frame = pltpu.VMEM((planes, width + 2 * lead, skip), jnp.float32)
    taps = pltpu.VMEM((depth + 2, height // 2 + 1, 2, width, 3 * skip), half)
    pairs = pltpu.VMEM((3, 4, 3, skip, 2 * skip), half)
    far = pl.BlockSpec(memory_space=pltpu.HBM)
    bias = lambda size: pltpu.VMEM((1, size), jnp.float32)
    return pl.pallas_call(
        functools.partial(kernel, sizes),
        out_shape=jax.ShapeDtypeStruct(volume.shape, half),
        in_specs=[far] * 11,
        out_specs=far,
        scratch_shapes=[
            cells,
            cells,
            cells,
            pltpu.VMEM((half_depth + 2, half_height + 2, half_width, deep), half),
            frame,
            frame,
            frame,
            pltpu.VMEM((deep // skip, low_planes, half_width + 2 * lead, skip), jnp.float32),
            taps,
            taps,
            taps,
            pltpu.VMEM((half_depth + 2, half_height + 2, half_width, 3 * deep), half),
            pltpu.VMEM((3, 2, planes, skip), half),
            pltpu.VMEM((3, 2, planes, skip), half),
            pltpu.VMEM((2, low_planes, deep), half),
            pltpu.VMEM((2, low_planes, deep), half),
            pairs,
            pairs,
            pairs,
            pltpu.VMEM(w_down.shape, half),
            pltpu.VMEM(w_bottom.shape, half),
            pltpu.VMEM((deep, 8 * skip), half),
            pltpu.VMEM((half_depth, half_height, half_width, 8 * skip), half),
            pltpu.VMEM((half_depth, height * width, 2 * skip), jnp.float32),
            pltpu.VMEM(volume.shape, half),
            bias(skip),
            bias(deep),
            bias(deep),
            bias(skip),
            bias(skip),
            pltpu.SemaphoreType.DMA((4, 8)),
            pltpu.SemaphoreType.DMA((4, 8)),
            pltpu.SemaphoreType.DMA((4, 2)),
            pltpu.SemaphoreType.DMA((4, 2)),
            pltpu.SemaphoreType.DMA((34,)),
            pltpu.SemaphoreType.DMA((half_depth,)),
        ],
        compiler_params=pltpu.CompilerParams(
            collective_id=0, has_side_effects=True, vmem_limit_bytes=63 * 2**20
        ),
    )(
        volume,
        w_encode,
        w_down,
        w_bottom,
        w_up,
        w_decode,
        b_encode.reshape(1, -1),
        b_down.reshape(1, -1),
        b_bottom.reshape(1, -1),
        b_up.reshape(1, -1),
        b_decode.reshape(1, -1),
    )


def solution(mesh):
    sizes = (mesh.shape["wide"], mesh.shape["narrow"], mesh.shape["pair"])
    placed = P(("groups", "wide"), "narrow", "pair", None)
    return jax.shard_map(
        functools.partial(body, sizes),
        mesh=mesh,
        in_specs=(placed,) + (P(),) * 10,
        out_specs=placed,
        check_vma=False,
    )
```

```python
import functools
import itertools

import jax
import jax.numpy as jnp
from jax import lax
from jax.experimental import pallas as pl
from jax.experimental.pallas import tpu as pltpu
from jax.sharding import PartitionSpec as P

leak_slope = 0.01
MESH = pl.DeviceIdType.MESH
lead = 8
corners = list(itertools.product((0, 1), repeat=2))
plane_steps = [s for s in itertools.product((-1, 0, 1), repeat=2) if s != (0, 0)]
width_steps = (-1, 1)


def leaky_relu(values):
    return jnp.maximum(values, leak_slope * values)


def rounded(values):
    return values.astype(jnp.bfloat16)


def whole_tiles(cells):
    return cells + -cells % 16


def source_span(step, cells, base):
    if step == 0:
        return pl.ds(base, cells)
    return pl.ds(base + (0 if step < 0 else cells - 1), 1)


def target_span(step, cells):
    if step == 0:
        return pl.ds(1, cells)
    return pl.ds(cells + 1 if step < 0 else 0, 1)


def kernel(
    sizes,
    volume,
    w_encode,
    w_down,
    w_bottom,
    w_up,
    w_decode,
    b_encode_far,
    b_down_far,
    b_bottom_far,
    b_up_far,
    b_decode_far,
    decoded,
    v_cells,
    e_cells,
    r_cells,
    c_cells,
    v_frame,
    e_frame,
    r_frame,
    c_frame,
    v_taps,
    e_taps,
    r_taps,
    c_taps,
    edge_out,
    edge_in,
    line_out,
    line_in,
    corner_in,
    c_edge_out,
    c_edge_in,
    c_line_out,
    c_line_in,
    c_corner_in,
    encode_pairs,
    skip_pairs,
    raised_pairs,
    down_matrix,
    bottom_matrix,
    up_matrix,
    down_rows,
    partial,
    result,
    b_encode,
    b_down,
    b_bottom,
    b_up,
    b_decode,
    send_sem,
    recv_sem,
    edge_send_sem,
    edge_recv_sem,
    load_sem,
    store_sem,
):
    depth, height, width, skip = volume.shape
    half_depth, half_height, half_width = depth // 2, height // 2, width // 2
    deep = w_down.shape[-1]
    deep_size, high_size, wide_size = sizes
    at_deep, at_high, at_wide = (lax.axis_index(name) for name in ("wide", "narrow", "pair"))

    def inside(place, step, size):
        return jnp.logical_and(place + step >= 0, place + step < size)

    def exists(step):
        return jnp.logical_and(
            jnp.logical_and(
                inside(at_deep, step[0], deep_size), inside(at_high, step[1], high_size)
            ),
            inside(at_wide, step[2], wide_size),
        )

    def place(step):
        return {"wide": at_deep + step[0], "narrow": at_high + step[1], "pair": at_wide + step[2]}

    plane_used = [
        s
        for s in plane_steps
        if (s[0] == 0 or deep_size > 1) and (s[1] == 0 or high_size > 1)
    ]
    width_used = width_steps if wide_size > 1 else ()
    all_used = [s + (0,) for s in plane_used]
    all_used += [s + (x,) for s in [(0, 0)] + plane_used for x in width_used]

    loads = []

    def load(source, target):
        copy = pltpu.make_async_copy(source, target, load_sem.at[len(loads)])
        copy.start()
        loads.append(copy)
        return copy

    own_load = load(volume, v_cells.at[pl.ds(1, depth), pl.ds(1, height)])

    def load_pairs(weight, first, target):
        return [
            load(
                weight.at[a, :, :, pl.ds(first, skip), :],
                target.at[a, pl.ds(j, 3), :, :, pl.ds(j * skip, skip)],
            )
            for a in range(3)
            for j in range(2)
        ]

    encode_loads = load_pairs(w_encode, 0, encode_pairs)
    encode_loads += [
        load(b_encode_far, b_encode),
        load(b_down_far, b_down),
        load(b_bottom_far, b_bottom),
        load(b_up_far, b_up),
        load(b_decode_far, b_decode),
    ]
    down_load = load(w_down, down_matrix)

    def zero_halo(cells, planes, rows):
        blank = jnp.zeros(cells.shape[2:], cells.dtype)
        for z in range(planes + 2):
            for y in range(rows + 2):
                if z in (0, planes + 1) or y in (0, rows + 1):
                    cells[z, y] = blank

    for cells in (v_cells, e_cells, r_cells):
        zero_halo(cells, depth, height)
    zero_halo(c_cells, half_depth, half_height)
    for arriving in (edge_in, line_in, corner_in, c_edge_in, c_line_in, c_corner_in):
        arriving[...] = jnp.zeros_like(arriving)

    barrier = pltpu.get_barrier_semaphore()
    for step in all_used:

        @pl.when(exists(step))
        def _():
            pl.semaphore_signal(barrier, inc=1, device_id=place(step), device_id_type=MESH)

    pl.semaphore_wait(barrier, sum(exists(step).astype(jnp.int32) for step in all_used))

    started = []

    def send(step, source, target, sends, receives):
        copy = pltpu.make_async_remote_copy(
            src_ref=source,
            dst_ref=target,
            send_sem=sends,
            recv_sem=receives,
            device_id=place(step),
            device_id_type=MESH,
        )
        pl.when(exists(step))(copy.start)
        started.append((exists(step), copy))
        return exists(tuple(-offset for offset in step)), copy

    def send_planes(slot, cells, source, base, planes, rows):
        return [
            send(
                step + (0,),
                source.at[source_span(step[0], planes, base), source_span(step[1], rows, base)],
                cells.at[target_span(step[0], planes), target_span(step[1], rows)],
                send_sem.at[slot, k],
                recv_sem.at[slot, k],
            )
            for k, step in enumerate(plane_used)
        ]

    def send_edges(slot, edges, lines, arriving, arriving_lines, arriving_corners, planes, rows):
        slab = whole_tiles(rows + 2)
        copies = []
        for n, step in enumerate([(0, 0)] + plane_used):
            for k, across in enumerate(width_used):
                if step[0] == 0:
                    here = there = pl.ds(slab, planes * slab)
                else:
                    here = pl.ds((1 if step[0] < 0 else planes) * slab, slab)
                    there = pl.ds((planes + 1 if step[0] < 0 else 0) * slab, slab)
                side = 1 if step[1] < 0 else 0
                if step[1] == 0:
                    source, target = edges.at[k, here], arriving.at[k, there]
                elif step[0] == 0:
                    source, target = lines.at[k, 1 - side], arriving_lines.at[k, side]
                else:
                    corner = corners.index((1 if step[0] < 0 else 0, side))
                    source, target = edges.at[k, here], arriving_corners.at[k, corner]
                copies.append(
                    send(
                        step + (across,),
                        source,
                        target,
                        edge_send_sem.at[slot, k, n],
                        edge_recv_sem.at[slot, k, n],
                    )
                )
        return copies

    def arrive(copies):
        for coming, copy in copies:
            pl.when(coming)(copy.wait_recv)

    def take_edges(frame, edges, lines, planes, rows, cells):
        slab = whole_tiles(rows + 2)
        count, pitch, channels = frame.shape
        flat = frame.reshape(count * pitch, channels)
        for k, column in enumerate((lead, lead + cells - 1)):
            edges[k] = rounded(flat[pl.ds(column, (planes + 2) * slab, stride=pitch), :])
            for j, y in enumerate((1, rows)):
                lines[k, j] = rounded(
                    flat[pl.ds(y * pitch + column, count // slab, stride=slab * pitch), :]
                )

    def put_edges(frame, arriving, arriving_lines, arriving_corners, planes, rows, cells):
        slab = whole_tiles(rows + 2)
        count, pitch, channels = frame.shape
        flat = frame.reshape(count * pitch, channels)
        for k, column in enumerate((lead + cells, lead - 1)):
            flat[pl.ds(column, (planes + 2) * slab, stride=pitch), :] = arriving[k].astype(
                jnp.float32
            )
            for j, y in enumerate((0, rows + 1)):
                flat[
                    pl.ds(y * pitch + column, count // slab, stride=slab * pitch), :
                ] = arriving_lines[k, j].astype(jnp.float32)
            for n, (deep_side, high_side) in enumerate(corners):
                plane = deep_side * (planes + 1) * slab + high_side * (rows + 1)
                row = 1 if high_side else rows
                frame[plane, column : column + 1, :] = arriving_corners[k, n].astype(jnp.float32)[
                    row : row + 1
                ]

    def lanes(h):
        return pl.ds(h * skip, skip)

    def halo_to_frame(cells, frame, planes, rows, span):
        for z in range(planes + 2):
            for y in range(rows + 2):
                if z in (0, planes + 1) or y in (0, rows + 1):
                    frame[z * whole_tiles(rows + 2) + y, lead : lead + span, :] = cells[z, y].astype(
                        jnp.float32
                    )

    deep_parts = range(deep // skip)

    slab = whole_tiles(height + 2)
    low_slab = whole_tiles(half_height + 2)
    middle = width // 2

    def spread(frame, taps, z, y, c, first, cells):
        begin = lead - 1 + c + first
        taps[z, y // 2, y % 2, first : first + cells, c * skip : (c + 1) * skip] = rounded(
            frame[z * slab + y, begin : begin + cells, :]
        )

    def spread_own(frame, taps):
        def one(z, carry):
            for y in range(1, height + 1):
                spread(frame, taps, z, y, 0, middle, middle)
                spread(frame, taps, z, y, 1, 0, width)
                spread(frame, taps, z, y, 2, 0, middle)
            return carry

        lax.fori_loop(1, depth + 1, one, 0)

    def spread_rest(frame, taps):
        def one(z, carry):
            for y in range(1, height + 1):
                spread(frame, taps, z, y, 0, 0, middle)
                spread(frame, taps, z, y, 2, middle, middle)
            for y, c in itertools.product((0, height + 1), range(3)):
                spread(frame, taps, z, y, c, 0, width)
            return carry

        lax.fori_loop(1, depth + 1, one, 0)
        for z in (0, depth + 1):
            for y, c in itertools.product(range(height + 2), range(3)):
                spread(frame, taps, z, y, c, 0, width)

    def pair_conv(taps, matrix, z):
        total = None
        for a in range(3):
            rows = jnp.concatenate(
                [
                    taps[pl.ds(z + a, 2), pl.ds(r // 2, half_height), r % 2].reshape(
                        2 * half_height * width, 3 * skip
                    )
                    for r in range(4)
                ],
                axis=-1,
            )
            term = jnp.dot(
                rows,
                matrix[a].reshape(12 * skip, 2 * skip),
                preferred_element_type=jnp.float32,
            )
            total = term if total is None else total + term
        return total

    v_copies = send_planes(0, v_cells, volume, 0, depth, height)
    own_load.wait()

    def widen(z, carry):
        for y in range(1, height + 1):
            v_frame[z * slab + y, lead : lead + width, :] = v_cells[z, y].astype(jnp.float32)
        return carry

    lax.fori_loop(1, depth + 1, widen, 0)

    def begin_edges(slot, frame, n):
        take_edges(frame, edge_out.at[n], line_out.at[n], depth, height, width)
        arriving = (edge_in.at[n], line_in.at[n], corner_in.at[n])
        copies = send_edges(
            slot, edge_out.at[n], line_out.at[n], *arriving, depth, height
        )
        return arriving, copies

    v_arriving, v_edges = begin_edges(0, v_frame, 0)
    bottom_load = load(w_bottom, bottom_matrix)
    skip_loads = load_pairs(w_decode, skip, skip_pairs)
    up_loads = [
        load(
            w_up.at[a, b, c],
            up_matrix.at[:, pl.ds(((a * 2 + b) * 2 + c) * skip, skip)],
        )
        for a, b, c in itertools.product((0, 1), repeat=3)
    ]
    raised_loads = load_pairs(w_decode, 0, raised_pairs)
    for pairs in (encode_pairs, skip_pairs, raised_pairs):
        for a in range(3):
            pairs[a, 0, :, :, skip : 2 * skip] = jnp.zeros((3, skip, skip), jnp.bfloat16)
            pairs[a, 3, :, :, 0:skip] = jnp.zeros((3, skip, skip), jnp.bfloat16)
    spread_own(v_frame, v_taps)
    arrive(v_copies)
    halo_to_frame(v_cells, v_frame, depth, height, width)
    arrive(v_edges)
    put_edges(v_frame, *v_arriving, depth, height, width)
    spread_rest(v_frame, v_taps)
    for copy in encode_loads:
        copy.wait()
    encode_bias = jnp.concatenate([b_encode[...], b_encode[...]], axis=-1)

    def encode(i, carry):
        z = 2 * i
        values = rounded(leaky_relu(pair_conv(v_taps, encode_pairs, z) + encode_bias))
        values = values.reshape(2, half_height, width, 2 * skip)
        for dz in range(2):
            for y in range(height):
                cells = values[dz, y // 2, :, (y % 2) * skip : (y % 2 + 1) * skip]
                e_cells[z + dz + 1, y + 1] = cells
                e_frame[(z + dz + 1) * slab + y + 1, lead : lead + width, :] = cells.astype(
                    jnp.float32
                )
        return carry

    lax.fori_loop(0, half_depth, encode, 0)

    def gather_down(z, carry):
        for y in range(half_height):
            for a, b, c in itertools.product((0, 1), repeat=3):
                tap = (a * 2 + b) * 2 + c
                down_rows[z, y, :, tap * skip : (tap + 1) * skip] = rounded(
                    e_frame[
                        (2 * z + a + 1) * slab + 2 * y + b + 1,
                        pl.ds(lead + c, half_width, stride=2),
                        :,
                    ]
                )
        return carry

    lax.fori_loop(0, half_depth, gather_down, 0)
    down_load.wait()
    low_cells = half_depth * half_height * half_width
    coarse = jnp.dot(
        down_rows[...].reshape(low_cells, 8 * skip),
        down_matrix[...].reshape(8 * skip, deep),
        preferred_element_type=jnp.float32,
    )
    coarse = rounded(leaky_relu(coarse + b_down[...]))
    coarse = coarse.reshape(half_depth, half_height, half_width, deep)
    c_cells[1 : 1 + half_depth, 1 : 1 + half_height] = coarse
    c_copies = send_planes(2, c_cells, c_cells, 1, half_depth, half_height)
    for z in range(half_depth):
        for y in range(half_height):
            for h in deep_parts:
                c_frame[
                    h, (z + 1) * low_slab + y + 1, lead : lead + half_width, :
                ] = coarse[z, y, :, h * skip : (h + 1) * skip].astype(jnp.float32)

    low = (half_depth, half_height, half_width)
    c_edges = []
    for h in deep_parts:
        take_edges(
            c_frame.at[h], c_edge_out.at[:, :, lanes(h)], c_line_out.at[:, :, :, lanes(h)], *low
        )
    c_edges = send_edges(
        2, c_edge_out, c_line_out, c_edge_in, c_line_in, c_corner_in, half_depth, half_height
    )
    e_copies = send_planes(1, e_cells, e_cells, 1, depth, height)
    e_arriving, e_edges = begin_edges(1, e_frame, 1)
    spread_own(e_frame, e_taps)

    def decode_skip(i):
        partial[i] = pair_conv(e_taps, skip_pairs, 2 * i)

    arrive(c_copies)
    for h in deep_parts:
        halo_to_frame(c_cells.at[:, :, :, lanes(h)], c_frame.at[h], *low)
    arrive(c_edges)
    for h in deep_parts:
        put_edges(
            c_frame.at[h],
            c_edge_in.at[:, :, lanes(h)],
            c_line_in.at[:, :, :, lanes(h)],
            c_corner_in.at[:, :, :, lanes(h)],
            *low,
        )
    for z in range(half_depth + 2):
        for y in range(half_height + 2):
            for c, h in itertools.product(range(3), deep_parts):
                first = c * deep + h * skip
                c_taps[z, y, :, first : first + skip] = rounded(
                    c_frame[
                        h, z * low_slab + y, lead - 1 + c : lead - 1 + c + half_width, :
                    ]
                )
    bottom_load.wait()
    total = jnp.zeros((low_cells, deep), jnp.float32)
    for a in range(3):
        for b in range(3):
            total += jnp.dot(
                c_taps[a : a + half_depth, b : b + half_height].reshape(low_cells, 3 * deep),
                bottom_matrix[a, b].reshape(3 * deep, deep),
                preferred_element_type=jnp.float32,
            )
    bottom = rounded(leaky_relu(total + b_bottom[...]))
    for copy in up_loads:
        copy.wait()
    up_bias = jnp.concatenate([b_up[...], b_up[...]], axis=-1)
    for a in range(2):
        for b in range(2):
            first = (a * 2 + b) * 2 * skip
            lifted = jnp.dot(
                bottom, up_matrix[:, first : first + 2 * skip], preferred_element_type=jnp.float32
            )
            lifted = rounded(lifted + up_bias).astype(jnp.float32)
            lifted = lifted.reshape(half_depth, half_height, half_width, 2 * skip)
            for z in range(half_depth):
                for y in range(half_height):
                    plane = (2 * z + a + 1) * slab + 2 * y + b + 1
                    for c in range(2):
                        r_frame[plane, pl.ds(lead + c, half_width, stride=2), :] = lifted[
                            z, y, :, c * skip : (c + 1) * skip
                        ]

    def narrow_raised(z, carry):
        for y in range(height):
            r_cells[z + 1, y + 1] = rounded(
                r_frame[(z + 1) * slab + y + 1, lead : lead + width, :]
            )
        return carry

    lax.fori_loop(0, depth, narrow_raised, 0)
    r_copies = send_planes(3, r_cells, r_cells, 1, depth, height)

    r_arriving, r_edges = begin_edges(3, r_frame, 2)
    spread_own(r_frame, r_taps)
    arrive(e_copies)
    halo_to_frame(e_cells, e_frame, depth, height, width)
    arrive(e_edges)
    put_edges(e_frame, *e_arriving, depth, height, width)
    spread_rest(e_frame, e_taps)
    for copy in skip_loads:
        copy.wait()
    for i in range(half_depth):
        decode_skip(i)
    arrive(r_copies)
    halo_to_frame(r_cells, r_frame, depth, height, width)
    arrive(r_edges)
    put_edges(r_frame, *r_arriving, depth, height, width)
    spread_rest(r_frame, r_taps)
    for copy in raised_loads:
        copy.wait()
    decode_bias = jnp.concatenate([b_decode[...], b_decode[...]], axis=-1)
    stores = []
    for i in range(half_depth):
        values = pair_conv(r_taps, raised_pairs, 2 * i) + partial[i]
        values = (values + decode_bias).reshape(2, half_height, width, 2 * skip)
        for dz in range(2):
            for y in range(height):
                result[2 * i + dz, y] = values[
                    dz, y // 2, :, (y % 2) * skip : (y % 2 + 1) * skip
                ]
        store = pltpu.make_async_copy(
            result.at[pl.ds(2 * i, 2)], decoded.at[pl.ds(2 * i, 2)], store_sem.at[i]
        )
        store.start()
        stores.append(store)
    for going, copy in started:
        pl.when(going)(copy.wait_send)
    for store in stores:
        store.wait()


def body(
    sizes,
    volume,
    w_encode,
    b_encode,
    w_down,
    b_down,
    w_bottom,
    b_bottom,
    w_up,
    b_up,
    w_decode,
    b_decode,
):
    depth, height, width, skip = volume.shape
    deep = w_down.shape[-1]
    half_depth, half_height, half_width = depth // 2, height // 2, width // 2
    planes, low_planes = depth + 2, half_depth + 2
    slab, low_slab = whole_tiles(height + 2), whole_tiles(half_height + 2)
    line, low_line = whole_tiles(planes), whole_tiles(low_planes)
    half = jnp.bfloat16
    cells = pltpu.VMEM((depth + 2, height + 2, width, skip), half)
    frame = pltpu.VMEM((line * slab, width + 2 * lead, skip), jnp.float32)
    taps = pltpu.VMEM((depth + 2, height // 2 + 1, 2, width, 3 * skip), half)
    pairs = pltpu.VMEM((3, 4, 3, skip, 2 * skip), half)
    far = pl.BlockSpec(memory_space=pltpu.HBM)
    bias = lambda size: pltpu.VMEM((1, size), jnp.float32)
    total = pl.pallas_call(
        functools.partial(kernel, sizes),
        out_shape=jax.ShapeDtypeStruct(volume.shape, jnp.float32),
        in_specs=[far] * 11,
        out_specs=far,
        scratch_shapes=[
            cells,
            cells,
            cells,
            pltpu.VMEM((half_depth + 2, half_height + 2, half_width, deep), half),
            frame,
            frame,
            frame,
            pltpu.VMEM((deep // skip, low_line * low_slab, half_width + 2 * lead, skip), jnp.float32),
            taps,
            taps,
            taps,
            pltpu.VMEM((half_depth + 2, half_height + 2, half_width, 3 * deep), half),
            pltpu.VMEM((3, 2, planes * slab, skip), half),
            pltpu.VMEM((3, 2, planes * slab, skip), half),
            pltpu.VMEM((3, 2, 2, line, skip), half),
            pltpu.VMEM((3, 2, 2, line, skip), half),
            pltpu.VMEM((3, 2, 4, slab, skip), half),
            pltpu.VMEM((2, low_planes * low_slab, deep), half),
            pltpu.VMEM((2, low_planes * low_slab, deep), half),
            pltpu.VMEM((2, 2, low_line, deep), half),
            pltpu.VMEM((2, 2, low_line, deep), half),
            pltpu.VMEM((2, 4, low_slab, deep), half),
            pairs,
            pairs,
            pairs,
            pltpu.VMEM(w_down.shape, half),
            pltpu.VMEM(w_bottom.shape, half),
            pltpu.VMEM((deep, 8 * skip), half),
            pltpu.VMEM((half_depth, half_height, half_width, 8 * skip), half),
            pltpu.VMEM((half_depth, height * width, 2 * skip), jnp.float32),
            pltpu.VMEM(volume.shape, jnp.float32),
            bias(skip),
            bias(deep),
            bias(deep),
            bias(skip),
            bias(skip),
            pltpu.SemaphoreType.DMA((4, 8)),
            pltpu.SemaphoreType.DMA((4, 8)),
            pltpu.SemaphoreType.DMA((4, 2, 9)),
            pltpu.SemaphoreType.DMA((4, 2, 9)),
            pltpu.SemaphoreType.DMA((34,)),
            pltpu.SemaphoreType.DMA((half_depth,)),
        ],
        compiler_params=pltpu.CompilerParams(
            collective_id=0, has_side_effects=True, vmem_limit_bytes=63 * 2**20
        ),
    )(
        volume,
        w_encode,
        w_down,
        w_bottom,
        w_up,
        w_decode,
        b_encode.reshape(1, -1),
        b_down.reshape(1, -1),
        b_bottom.reshape(1, -1),
        b_up.reshape(1, -1),
        b_decode.reshape(1, -1),
    )
    return rounded(leaky_relu(total))


def solution(mesh):
    sizes = (mesh.shape["wide"], mesh.shape["narrow"], mesh.shape["pair"])
    placed = P(("groups", "wide"), "narrow", "pair", None)
    return jax.shard_map(
        functools.partial(body, sizes),
        mesh=mesh,
        in_specs=(placed,) + (P(),) * 10,
        out_specs=placed,
        check_vma=False,
    )
```

```python
import functools
import itertools

import jax
import jax.numpy as jnp
from jax import lax
from jax.experimental import pallas as pl
from jax.experimental.pallas import tpu as pltpu
from jax.sharding import PartitionSpec as P

leak_slope = 0.01
MESH = pl.DeviceIdType.MESH
lead = 8
corners = list(itertools.product((0, 1), repeat=2))
plane_steps = [s for s in itertools.product((-1, 0, 1), repeat=2) if s != (0, 0)]
width_steps = (-1, 1)


def leaky_relu(values):
    return jnp.maximum(values, leak_slope * values)


def rounded(values):
    return values.astype(jnp.bfloat16)


def whole_tiles(cells):
    return cells + -cells % 16


def source_span(step, cells, base):
    if step == 0:
        return pl.ds(base, cells)
    return pl.ds(base + (0 if step < 0 else cells - 1), 1)


def target_span(step, cells):
    if step == 0:
        return pl.ds(1, cells)
    return pl.ds(cells + 1 if step < 0 else 0, 1)


def kernel(
    sizes,
    volume,
    w_encode,
    w_down,
    w_bottom,
    w_up,
    w_decode,
    b_encode_far,
    b_down_far,
    b_bottom_far,
    b_up_far,
    b_decode_far,
    decoded,
    v_cells,
    e_cells,
    r_cells,
    c_cells,
    v_frame,
    e_frame,
    r_frame,
    c_frame,
    v_taps,
    e_taps,
    r_taps,
    c_taps,
    edge_out,
    edge_in,
    line_out,
    line_in,
    corner_in,
    c_edge_out,
    c_edge_in,
    c_line_out,
    c_line_in,
    c_corner_in,
    encode_pairs,
    skip_pairs,
    raised_pairs,
    down_matrix,
    bottom_matrix,
    up_matrix,
    down_rows,
    partial,
    result,
    b_encode,
    b_down,
    b_bottom,
    b_up,
    b_decode,
    send_sem,
    recv_sem,
    edge_send_sem,
    edge_recv_sem,
    load_sem,
    store_sem,
):
    depth, height, width, skip = volume.shape
    half_depth, half_height, half_width = depth // 2, height // 2, width // 2
    deep = w_down.shape[-1]
    deep_size, high_size, wide_size = sizes
    at_deep, at_high, at_wide = (lax.axis_index(name) for name in ("wide", "narrow", "pair"))

    def inside(place, step, size):
        return jnp.logical_and(place + step >= 0, place + step < size)

    def exists(step):
        return jnp.logical_and(
            jnp.logical_and(
                inside(at_deep, step[0], deep_size), inside(at_high, step[1], high_size)
            ),
            inside(at_wide, step[2], wide_size),
        )

    def place(step):
        return {"wide": at_deep + step[0], "narrow": at_high + step[1], "pair": at_wide + step[2]}

    plane_used = [
        s
        for s in plane_steps
        if (s[0] == 0 or deep_size > 1) and (s[1] == 0 or high_size > 1)
    ]
    width_used = width_steps if wide_size > 1 else ()
    all_used = [s + (0,) for s in plane_used]
    all_used += [s + (x,) for s in [(0, 0)] + plane_used for x in width_used]

    loads = []

    def load(source, target):
        copy = pltpu.make_async_copy(source, target, load_sem.at[len(loads)])
        copy.start()
        loads.append(copy)
        return copy

    own_load = load(volume, v_cells.at[pl.ds(1, depth), pl.ds(1, height)])

    def load_pairs(weight, first, target):
        return [
            load(
                weight.at[a, :, :, pl.ds(first, skip), :],
                target.at[a, pl.ds(j, 3), :, :, pl.ds(j * skip, skip)],
            )
            for a in range(3)
            for j in range(2)
        ]

    encode_loads = load_pairs(w_encode, 0, encode_pairs)
    encode_loads += [
        load(b_encode_far, b_encode),
        load(b_down_far, b_down),
        load(b_bottom_far, b_bottom),
        load(b_up_far, b_up),
        load(b_decode_far, b_decode),
    ]
    down_load = load(w_down, down_matrix)

    def zero_halo(cells, planes, rows):
        blank = jnp.zeros(cells.shape[2:], cells.dtype)
        for z in range(planes + 2):
            for y in range(rows + 2):
                if z in (0, planes + 1) or y in (0, rows + 1):
                    cells[z, y] = blank

    for cells in (v_cells, e_cells, r_cells):
        zero_halo(cells, depth, height)
    zero_halo(c_cells, half_depth, half_height)
    for arriving in (edge_in, line_in, corner_in, c_edge_in, c_line_in, c_corner_in):
        arriving[...] = jnp.zeros_like(arriving)

    barrier = pltpu.get_barrier_semaphore()
    for step in all_used:

        @pl.when(exists(step))
        def _():
            pl.semaphore_signal(barrier, inc=1, device_id=place(step), device_id_type=MESH)

    pl.semaphore_wait(barrier, sum(exists(step).astype(jnp.int32) for step in all_used))

    started = []

    def send(step, source, target, sends, receives):
        copy = pltpu.make_async_remote_copy(
            src_ref=source,
            dst_ref=target,
            send_sem=sends,
            recv_sem=receives,
            device_id=place(step),
            device_id_type=MESH,
        )
        pl.when(exists(step))(copy.start)
        started.append((exists(step), copy))
        return exists(tuple(-offset for offset in step)), copy

    def send_planes(slot, cells, source, base, planes, rows):
        return [
            send(
                step + (0,),
                source.at[source_span(step[0], planes, base), source_span(step[1], rows, base)],
                cells.at[target_span(step[0], planes), target_span(step[1], rows)],
                send_sem.at[slot, k],
                recv_sem.at[slot, k],
            )
            for k, step in enumerate(plane_used)
        ]

    def send_edges(slot, edges, lines, arriving, arriving_lines, arriving_corners, planes, rows):
        slab = whole_tiles(rows + 2)
        copies = []
        for n, step in enumerate([(0, 0)] + plane_used):
            for k, across in enumerate(width_used):
                if step[0] == 0:
                    here = there = pl.ds(slab, planes * slab)
                else:
                    here = pl.ds((1 if step[0] < 0 else planes) * slab, slab)
                    there = pl.ds((planes + 1 if step[0] < 0 else 0) * slab, slab)
                side = 1 if step[1] < 0 else 0
                if step[1] == 0:
                    source, target = edges.at[k, here], arriving.at[k, there]
                elif step[0] == 0:
                    source, target = lines.at[k, 1 - side], arriving_lines.at[k, side]
                else:
                    corner = corners.index((1 if step[0] < 0 else 0, side))
                    source, target = edges.at[k, here], arriving_corners.at[k, corner]
                copies.append(
                    send(
                        step + (across,),
                        source,
                        target,
                        edge_send_sem.at[slot, k, n],
                        edge_recv_sem.at[slot, k, n],
                    )
                )
        return copies

    def arrive(copies):
        for coming, copy in copies:
            pl.when(coming)(copy.wait_recv)

    def take_edges(frame, edges, lines, planes, rows, cells):
        slab = whole_tiles(rows + 2)
        count, pitch, channels = frame.shape
        flat = frame.reshape(count * pitch, channels)
        for k, column in enumerate((lead, lead + cells - 1)):
            edges[k] = rounded(flat[pl.ds(column, (planes + 2) * slab, stride=pitch), :])
            for j, y in enumerate((1, rows)):
                lines[k, j] = rounded(
                    flat[pl.ds(y * pitch + column, count // slab, stride=slab * pitch), :]
                )

    def put_edges(frame, arriving, arriving_lines, arriving_corners, planes, rows, cells):
        slab = whole_tiles(rows + 2)
        count, pitch, channels = frame.shape
        flat = frame.reshape(count * pitch, channels)
        for k, column in enumerate((lead + cells, lead - 1)):
            flat[pl.ds(column, (planes + 2) * slab, stride=pitch), :] = arriving[k].astype(
                jnp.float32
            )
            for j, y in enumerate((0, rows + 1)):
                flat[
                    pl.ds(y * pitch + column, count // slab, stride=slab * pitch), :
                ] = arriving_lines[k, j].astype(jnp.float32)
            for n, (deep_side, high_side) in enumerate(corners):
                plane = deep_side * (planes + 1) * slab + high_side * (rows + 1)
                row = 1 if high_side else rows
                frame[plane, column : column + 1, :] = arriving_corners[k, n].astype(jnp.float32)[
                    row : row + 1
                ]

    def lanes(h):
        return pl.ds(h * skip, skip)

    def halo_to_frame(cells, frame, planes, rows, span):
        for z in range(planes + 2):
            for y in range(rows + 2):
                if z in (0, planes + 1) or y in (0, rows + 1):
                    frame[z * whole_tiles(rows + 2) + y, lead : lead + span, :] = cells[z, y].astype(
                        jnp.float32
                    )

    deep_parts = range(deep // skip)

    slab = whole_tiles(height + 2)
    low_slab = whole_tiles(half_height + 2)
    middle = width // 2

    def spread(frame, taps, z, y, c, first, cells):
        begin = lead - 1 + c + first
        taps[z, y // 2, y % 2, first : first + cells, c * skip : (c + 1) * skip] = rounded(
            frame[z * slab + y, begin : begin + cells, :]
        )

    def spread_own(frame, taps):
        def one(z, carry):
            for y in range(1, height + 1):
                spread(frame, taps, z, y, 0, middle, middle)
                spread(frame, taps, z, y, 1, 0, width)
                spread(frame, taps, z, y, 2, 0, middle)
            return carry

        lax.fori_loop(1, depth + 1, one, 0)

    def spread_rest(frame, taps):
        def one(z, carry):
            for y in range(1, height + 1):
                spread(frame, taps, z, y, 0, 0, middle)
                spread(frame, taps, z, y, 2, middle, middle)
            for y, c in itertools.product((0, height + 1), range(3)):
                spread(frame, taps, z, y, c, 0, width)
            return carry

        lax.fori_loop(1, depth + 1, one, 0)
        for z in (0, depth + 1):
            for y, c in itertools.product(range(height + 2), range(3)):
                spread(frame, taps, z, y, c, 0, width)

    def pair_conv(taps, matrix, fresh):
        for a in range(3):
            rows = jnp.concatenate(
                [
                    taps[a : a + depth, r // 2 : r // 2 + half_height, r % 2].reshape(
                        depth * half_height * width, 3 * skip
                    )
                    for r in range(4)
                ],
                axis=-1,
            )
            term = jnp.dot(
                rows,
                matrix[a].reshape(12 * skip, 2 * skip),
                preferred_element_type=jnp.float32,
            )
            if a == 0 and fresh:
                partial[...] = term
            else:
                partial[...] += term

    v_copies = send_planes(0, v_cells, volume, 0, depth, height)
    own_load.wait()

    def widen(z, carry):
        for y in range(1, height + 1):
            v_frame[z * slab + y, lead : lead + width, :] = v_cells[z, y].astype(jnp.float32)
        return carry

    lax.fori_loop(1, depth + 1, widen, 0)

    def begin_edges(slot, frame, n):
        take_edges(frame, edge_out.at[n], line_out.at[n], depth, height, width)
        arriving = (edge_in.at[n], line_in.at[n], corner_in.at[n])
        copies = send_edges(
            slot, edge_out.at[n], line_out.at[n], *arriving, depth, height
        )
        return arriving, copies

    v_arriving, v_edges = begin_edges(0, v_frame, 0)
    bottom_load = load(w_bottom, bottom_matrix)
    skip_loads = load_pairs(w_decode, skip, skip_pairs)
    up_loads = [
        load(
            w_up.at[a, b, c],
            up_matrix.at[:, pl.ds(((a * 2 + b) * 2 + c) * skip, skip)],
        )
        for a, b, c in itertools.product((0, 1), repeat=3)
    ]
    raised_loads = load_pairs(w_decode, 0, raised_pairs)
    for pairs in (encode_pairs, skip_pairs, raised_pairs):
        for a in range(3):
            pairs[a, 0, :, :, skip : 2 * skip] = jnp.zeros((3, skip, skip), jnp.bfloat16)
            pairs[a, 3, :, :, 0:skip] = jnp.zeros((3, skip, skip), jnp.bfloat16)
    spread_own(v_frame, v_taps)
    arrive(v_copies)
    halo_to_frame(v_cells, v_frame, depth, height, width)
    arrive(v_edges)
    put_edges(v_frame, *v_arriving, depth, height, width)
    spread_rest(v_frame, v_taps)
    for copy in encode_loads:
        copy.wait()
    encode_bias = jnp.concatenate([b_encode[...], b_encode[...]], axis=-1)

    pair_conv(v_taps, encode_pairs, True)
    sheet = half_height * width

    def encode(z, carry):
        values = partial[pl.ds(pl.multiple_of(z * sheet, sheet), sheet), :]
        values = rounded(leaky_relu(values + encode_bias))
        values = values.reshape(half_height, width, 2 * skip)
        for y in range(height):
            cells = values[y // 2, :, (y % 2) * skip : (y % 2 + 1) * skip]
            e_cells[z + 1, y + 1] = cells
            e_frame[(z + 1) * slab + y + 1, lead : lead + width, :] = cells.astype(jnp.float32)
        return carry

    lax.fori_loop(0, depth, encode, 0)

    def gather_down(z, carry):
        for y in range(half_height):
            for a, b, c in itertools.product((0, 1), repeat=3):
                tap = (a * 2 + b) * 2 + c
                down_rows[z, y, :, tap * skip : (tap + 1) * skip] = rounded(
                    e_frame[
                        (2 * z + a + 1) * slab + 2 * y + b + 1,
                        pl.ds(lead + c, half_width, stride=2),
                        :,
                    ]
                )
        return carry

    lax.fori_loop(0, half_depth, gather_down, 0)
    down_load.wait()
    low_cells = half_depth * half_height * half_width
    coarse = jnp.dot(
        down_rows[...].reshape(low_cells, 8 * skip),
        down_matrix[...].reshape(8 * skip, deep),
        preferred_element_type=jnp.float32,
    )
    coarse = rounded(leaky_relu(coarse + b_down[...]))
    coarse = coarse.reshape(half_depth, half_height, half_width, deep)
    c_cells[1 : 1 + half_depth, 1 : 1 + half_height] = coarse
    c_copies = send_planes(2, c_cells, c_cells, 1, half_depth, half_height)
    for z in range(half_depth):
        for y in range(half_height):
            for h in deep_parts:
                c_frame[
                    h, (z + 1) * low_slab + y + 1, lead : lead + half_width, :
                ] = coarse[z, y, :, h * skip : (h + 1) * skip].astype(jnp.float32)

    low = (half_depth, half_height, half_width)
    c_edges = []
    for h in deep_parts:
        take_edges(
            c_frame.at[h], c_edge_out.at[:, :, lanes(h)], c_line_out.at[:, :, :, lanes(h)], *low
        )
    c_edges = send_edges(
        2, c_edge_out, c_line_out, c_edge_in, c_line_in, c_corner_in, half_depth, half_height
    )
    e_copies = send_planes(1, e_cells, e_cells, 1, depth, height)
    e_arriving, e_edges = begin_edges(1, e_frame, 1)
    spread_own(e_frame, e_taps)

    arrive(c_copies)
    for h in deep_parts:
        halo_to_frame(c_cells.at[:, :, :, lanes(h)], c_frame.at[h], *low)
    arrive(c_edges)
    for h in deep_parts:
        put_edges(
            c_frame.at[h],
            c_edge_in.at[:, :, lanes(h)],
            c_line_in.at[:, :, :, lanes(h)],
            c_corner_in.at[:, :, :, lanes(h)],
            *low,
        )
    for z in range(half_depth + 2):
        for y in range(half_height + 2):
            for c, h in itertools.product(range(3), deep_parts):
                first = c * deep + h * skip
                c_taps[z, y, :, first : first + skip] = rounded(
                    c_frame[
                        h, z * low_slab + y, lead - 1 + c : lead - 1 + c + half_width, :
                    ]
                )
    bottom_load.wait()
    total = jnp.zeros((low_cells, deep), jnp.float32)
    for a in range(3):
        for b in range(3):
            total += jnp.dot(
                c_taps[a : a + half_depth, b : b + half_height].reshape(low_cells, 3 * deep),
                bottom_matrix[a, b].reshape(3 * deep, deep),
                preferred_element_type=jnp.float32,
            )
    bottom = rounded(leaky_relu(total + b_bottom[...]))
    for copy in up_loads:
        copy.wait()
    up_bias = jnp.concatenate([b_up[...], b_up[...]], axis=-1)
    for a in range(2):
        for b in range(2):
            first = (a * 2 + b) * 2 * skip
            lifted = jnp.dot(
                bottom, up_matrix[:, first : first + 2 * skip], preferred_element_type=jnp.float32
            )
            lifted = rounded(lifted + up_bias).astype(jnp.float32)
            lifted = lifted.reshape(half_depth, half_height, half_width, 2 * skip)
            for z in range(half_depth):
                for y in range(half_height):
                    plane = (2 * z + a + 1) * slab + 2 * y + b + 1
                    for c in range(2):
                        r_frame[plane, pl.ds(lead + c, half_width, stride=2), :] = lifted[
                            z, y, :, c * skip : (c + 1) * skip
                        ]

    def narrow_raised(z, carry):
        for y in range(height):
            r_cells[z + 1, y + 1] = rounded(
                r_frame[(z + 1) * slab + y + 1, lead : lead + width, :]
            )
        return carry

    lax.fori_loop(0, depth, narrow_raised, 0)
    r_copies = send_planes(3, r_cells, r_cells, 1, depth, height)

    r_arriving, r_edges = begin_edges(3, r_frame, 2)
    spread_own(r_frame, r_taps)
    arrive(e_copies)
    halo_to_frame(e_cells, e_frame, depth, height, width)
    arrive(e_edges)
    put_edges(e_frame, *e_arriving, depth, height, width)
    spread_rest(e_frame, e_taps)
    for copy in skip_loads:
        copy.wait()
    pair_conv(e_taps, skip_pairs, True)
    arrive(r_copies)
    halo_to_frame(r_cells, r_frame, depth, height, width)
    arrive(r_edges)
    put_edges(r_frame, *r_arriving, depth, height, width)
    spread_rest(r_frame, r_taps)
    for copy in raised_loads:
        copy.wait()
    decode_bias = jnp.concatenate([b_decode[...], b_decode[...]], axis=-1)
    pair_conv(r_taps, raised_pairs, False)

    def finish(z, carry):
        values = partial[pl.ds(pl.multiple_of(z * sheet, sheet), sheet), :]
        values = (values + decode_bias).reshape(half_height, width, 2 * skip)
        for y in range(height):
            result[z, y] = values[y // 2, :, (y % 2) * skip : (y % 2 + 1) * skip]
        return carry

    lax.fori_loop(0, depth, finish, 0)
    store = pltpu.make_async_copy(result, decoded, store_sem)
    store.start()
    for going, copy in started:
        pl.when(going)(copy.wait_send)
    store.wait()


def body(
    sizes,
    volume,
    w_encode,
    b_encode,
    w_down,
    b_down,
    w_bottom,
    b_bottom,
    w_up,
    b_up,
    w_decode,
    b_decode,
):
    depth, height, width, skip = volume.shape
    deep = w_down.shape[-1]
    half_depth, half_height, half_width = depth // 2, height // 2, width // 2
    planes, low_planes = depth + 2, half_depth + 2
    slab, low_slab = whole_tiles(height + 2), whole_tiles(half_height + 2)
    line, low_line = whole_tiles(planes), whole_tiles(low_planes)
    half = jnp.bfloat16
    cells = pltpu.VMEM((depth + 2, height + 2, width, skip), half)
    frame = pltpu.VMEM((line * slab, width + 2 * lead, skip), jnp.float32)
    taps = pltpu.VMEM((depth + 2, height // 2 + 1, 2, width, 3 * skip), half)
    pairs = pltpu.VMEM((3, 4, 3, skip, 2 * skip), half)
    far = pl.BlockSpec(memory_space=pltpu.HBM)
    bias = lambda size: pltpu.VMEM((1, size), jnp.float32)
    total = pl.pallas_call(
        functools.partial(kernel, sizes),
        out_shape=jax.ShapeDtypeStruct(volume.shape, jnp.float32),
        in_specs=[far] * 11,
        out_specs=far,
        scratch_shapes=[
            cells,
            cells,
            cells,
            pltpu.VMEM((half_depth + 2, half_height + 2, half_width, deep), half),
            frame,
            frame,
            frame,
            pltpu.VMEM((deep // skip, low_line * low_slab, half_width + 2 * lead, skip), jnp.float32),
            taps,
            taps,
            taps,
            pltpu.VMEM((half_depth + 2, half_height + 2, half_width, 3 * deep), half),
            pltpu.VMEM((3, 2, planes * slab, skip), half),
            pltpu.VMEM((3, 2, planes * slab, skip), half),
            pltpu.VMEM((3, 2, 2, line, skip), half),
            pltpu.VMEM((3, 2, 2, line, skip), half),
            pltpu.VMEM((3, 2, 4, slab, skip), half),
            pltpu.VMEM((2, low_planes * low_slab, deep), half),
            pltpu.VMEM((2, low_planes * low_slab, deep), half),
            pltpu.VMEM((2, 2, low_line, deep), half),
            pltpu.VMEM((2, 2, low_line, deep), half),
            pltpu.VMEM((2, 4, low_slab, deep), half),
            pairs,
            pairs,
            pairs,
            pltpu.VMEM(w_down.shape, half),
            pltpu.VMEM(w_bottom.shape, half),
            pltpu.VMEM((deep, 8 * skip), half),
            pltpu.VMEM((half_depth, half_height, half_width, 8 * skip), half),
            pltpu.VMEM((depth * height * width // 2, 2 * skip), jnp.float32),
            pltpu.VMEM(volume.shape, jnp.float32),
            bias(skip),
            bias(deep),
            bias(deep),
            bias(skip),
            bias(skip),
            pltpu.SemaphoreType.DMA((4, 8)),
            pltpu.SemaphoreType.DMA((4, 8)),
            pltpu.SemaphoreType.DMA((4, 2, 9)),
            pltpu.SemaphoreType.DMA((4, 2, 9)),
            pltpu.SemaphoreType.DMA((34,)),
            pltpu.SemaphoreType.DMA,
        ],
        compiler_params=pltpu.CompilerParams(
            collective_id=0, has_side_effects=True, vmem_limit_bytes=63 * 2**20
        ),
    )(
        volume,
        w_encode,
        w_down,
        w_bottom,
        w_up,
        w_decode,
        b_encode.reshape(1, -1),
        b_down.reshape(1, -1),
        b_bottom.reshape(1, -1),
        b_up.reshape(1, -1),
        b_decode.reshape(1, -1),
    )
    return rounded(leaky_relu(total))


def solution(mesh):
    sizes = (mesh.shape["wide"], mesh.shape["narrow"], mesh.shape["pair"])
    placed = P(("groups", "wide"), "narrow", "pair", None)
    return jax.shard_map(
        functools.partial(body, sizes),
        mesh=mesh,
        in_specs=(placed,) + (P(),) * 10,
        out_specs=placed,
        check_vma=False,
    )
```

```python
import functools
import itertools

import jax
import jax.numpy as jnp
from jax import lax
from jax.experimental import pallas as pl
from jax.experimental.pallas import tpu as pltpu
from jax.sharding import PartitionSpec as P

leak_slope = 0.01
MESH = pl.DeviceIdType.MESH
lead = 8
corners = list(itertools.product((0, 1), repeat=2))
plane_steps = [s for s in itertools.product((-1, 0, 1), repeat=2) if s != (0, 0)]
width_steps = (-1, 1)


def leaky_relu(values):
    return jnp.maximum(values, leak_slope * values)


def rounded(values):
    return values.astype(jnp.bfloat16)


def whole_tiles(cells):
    return cells + -cells % 16


def source_span(step, cells, base):
    if step == 0:
        return pl.ds(base, cells)
    return pl.ds(base + (0 if step < 0 else cells - 1), 1)


def target_span(step, cells):
    if step == 0:
        return pl.ds(1, cells)
    return pl.ds(cells + 1 if step < 0 else 0, 1)


def kernel(
    sizes,
    volume,
    w_encode,
    w_down,
    w_bottom,
    w_up,
    w_decode,
    b_encode_far,
    b_down_far,
    b_bottom_far,
    b_up_far,
    b_decode_far,
    decoded,
    v_cells,
    e_cells,
    r_cells,
    c_cells,
    v_frame,
    e_frame,
    r_frame,
    c_frame,
    v_taps,
    e_taps,
    r_taps,
    c_taps,
    edge_out,
    edge_in,
    line_out,
    line_in,
    corner_in,
    c_edge_out,
    c_edge_in,
    c_line_out,
    c_line_in,
    c_corner_in,
    encode_pairs,
    skip_pairs,
    raised_pairs,
    down_matrix,
    bottom_matrix,
    up_matrix,
    down_rows,
    partial,
    b_encode,
    b_down,
    b_bottom,
    b_up,
    b_decode,
    send_sem,
    recv_sem,
    edge_send_sem,
    edge_recv_sem,
    load_sem,
):
    depth, height, width, skip = volume.shape
    half_depth, half_height, half_width = depth // 2, height // 2, width // 2
    deep = w_down.shape[-1]
    deep_size, high_size, wide_size = sizes
    at_deep, at_high, at_wide = (lax.axis_index(name) for name in ("wide", "narrow", "pair"))

    def inside(place, step, size):
        return jnp.logical_and(place + step >= 0, place + step < size)

    def exists(step):
        near = jnp.logical_and(
            inside(at_deep, step[0], deep_size), inside(at_high, step[1], high_size)
        )
        if step[2] is None:
            return near
        return jnp.logical_and(near, inside(at_wide, step[2], wide_size))

    def reverse(step):
        return tuple(None if offset is None else -offset for offset in step)

    def place(step):
        column = 1 - at_wide if step[2] is None else at_wide + step[2]
        return {"wide": at_deep + step[0], "narrow": at_high + step[1], "pair": column}

    plane_used = [
        s
        for s in plane_steps
        if (s[0] == 0 or deep_size > 1) and (s[1] == 0 or high_size > 1)
    ]
    if wide_size == 2:
        width_used = ((None, 1 - at_wide),)
    else:
        width_used = tuple(zip(width_steps, (0, 1))) if wide_size > 1 else ()
    all_used = [s + (0,) for s in plane_used]
    all_used += [s + (x,) for s in [(0, 0)] + plane_used for x, _ in width_used]

    loads = []

    def load(source, target):
        copy = pltpu.make_async_copy(source, target, load_sem.at[len(loads)])
        copy.start()
        loads.append(copy)
        return copy

    own_load = load(volume, v_cells.at[pl.ds(1, depth), pl.ds(1, height)])

    def load_pairs(weight, first, target):
        return [
            load(
                weight.at[a, :, :, pl.ds(first, skip), :],
                target.at[a, pl.ds(j, 3), :, :, pl.ds(j * skip, skip)],
            )
            for a in range(3)
            for j in range(2)
        ]

    encode_loads = load_pairs(w_encode, 0, encode_pairs)
    encode_loads += [
        load(b_encode_far, b_encode),
        load(b_down_far, b_down),
        load(b_bottom_far, b_bottom),
        load(b_up_far, b_up),
        load(b_decode_far, b_decode),
    ]
    down_load = load(w_down, down_matrix)

    def zero_halo(cells, planes, rows):
        blank = jnp.zeros(cells.shape[2:], cells.dtype)
        for z in range(planes + 2):
            for y in range(rows + 2):
                if z in (0, planes + 1) or y in (0, rows + 1):
                    cells[z, y] = blank

    for cells in (v_cells, e_cells, r_cells):
        zero_halo(cells, depth, height)
    zero_halo(c_cells, half_depth, half_height)
    for arriving in (edge_in, line_in, corner_in, c_edge_in, c_line_in, c_corner_in):
        arriving[...] = jnp.zeros_like(arriving)

    barrier = pltpu.get_barrier_semaphore()
    for step in all_used:

        @pl.when(exists(step))
        def _():
            pl.semaphore_signal(barrier, inc=1, device_id=place(step), device_id_type=MESH)

    pl.semaphore_wait(barrier, sum(exists(step).astype(jnp.int32) for step in all_used))

    started = []

    def send(step, source, target, sends, receives):
        copy = pltpu.make_async_remote_copy(
            src_ref=source,
            dst_ref=target,
            send_sem=sends,
            recv_sem=receives,
            device_id=place(step),
            device_id_type=MESH,
        )
        pl.when(exists(step))(copy.start)
        started.append((exists(step), copy))
        return exists(reverse(step)), copy

    def send_planes(slot, cells, source, base, planes, rows):
        return [
            send(
                step + (0,),
                source.at[source_span(step[0], planes, base), source_span(step[1], rows, base)],
                cells.at[target_span(step[0], planes), target_span(step[1], rows)],
                send_sem.at[slot, k],
                recv_sem.at[slot, k],
            )
            for k, step in enumerate(plane_used)
        ]

    def send_edges(slot, edges, lines, arriving, arriving_lines, arriving_corners, planes, rows):
        slab = whole_tiles(rows + 2)
        copies = []
        for n, step in enumerate([(0, 0)] + plane_used):
            for lane, (across, k) in enumerate(width_used):
                if step[0] == 0:
                    here = there = pl.ds(slab, planes * slab)
                else:
                    here = pl.ds((1 if step[0] < 0 else planes) * slab, slab)
                    there = pl.ds((planes + 1 if step[0] < 0 else 0) * slab, slab)
                side = 1 if step[1] < 0 else 0
                if step[1] == 0:
                    source, target = edges.at[k, here], arriving.at[k, there]
                elif step[0] == 0:
                    source, target = lines.at[k, 1 - side], arriving_lines.at[k, side]
                else:
                    corner = corners.index((1 if step[0] < 0 else 0, side))
                    source, target = edges.at[k, here], arriving_corners.at[k, corner]
                copies.append(
                    send(
                        step + (across,),
                        source,
                        target,
                        edge_send_sem.at[slot, lane, n],
                        edge_recv_sem.at[slot, lane, n],
                    )
                )
        return copies

    def arrive(copies):
        for coming, copy in copies:
            pl.when(coming)(copy.wait_recv)

    def take_edges(frame, edges, lines, planes, rows, cells):
        slab = whole_tiles(rows + 2)
        count, pitch, channels = frame.shape
        flat = frame.reshape(count * pitch, channels)
        for k, column in enumerate((lead, lead + cells - 1)):
            edges[k] = rounded(flat[pl.ds(column, (planes + 2) * slab, stride=pitch), :])
            for j, y in enumerate((1, rows)):
                lines[k, j] = rounded(
                    flat[pl.ds(y * pitch + column, count // slab, stride=slab * pitch), :]
                )

    def put_edges(frame, arriving, arriving_lines, arriving_corners, planes, rows, cells):
        slab = whole_tiles(rows + 2)
        count, pitch, channels = frame.shape
        flat = frame.reshape(count * pitch, channels)
        for k, column in enumerate((lead + cells, lead - 1)):
            flat[pl.ds(column, (planes + 2) * slab, stride=pitch), :] = arriving[k].astype(
                jnp.float32
            )
            for j, y in enumerate((0, rows + 1)):
                flat[
                    pl.ds(y * pitch + column, count // slab, stride=slab * pitch), :
                ] = arriving_lines[k, j].astype(jnp.float32)
            for n, (deep_side, high_side) in enumerate(corners):
                plane = deep_side * (planes + 1) * slab + high_side * (rows + 1)
                row = 1 if high_side else rows
                frame[plane, column : column + 1, :] = arriving_corners[k, n].astype(jnp.float32)[
                    row : row + 1
                ]

    def lanes(h):
        return pl.ds(h * skip, skip)

    def halo_to_frame(cells, frame, planes, rows, span):
        for z in range(planes + 2):
            for y in range(rows + 2):
                if z in (0, planes + 1) or y in (0, rows + 1):
                    frame[z * whole_tiles(rows + 2) + y, lead : lead + span, :] = cells[z, y].astype(
                        jnp.float32
                    )

    deep_parts = range(deep // skip)

    slab = whole_tiles(height + 2)
    low_slab = whole_tiles(half_height + 2)
    middle = width // 2

    def spread(frame, taps, z, y, c, first, cells):
        begin = lead - 1 + c + first
        taps[z, y // 2, y % 2, first : first + cells, c * skip : (c + 1) * skip] = rounded(
            frame[z * slab + y, begin : begin + cells, :]
        )

    def spread_own(frame, taps):
        def one(z, carry):
            for y in range(1, height + 1):
                spread(frame, taps, z, y, 0, middle, middle)
                spread(frame, taps, z, y, 1, 0, width)
                spread(frame, taps, z, y, 2, 0, middle)
            return carry

        lax.fori_loop(1, depth + 1, one, 0)

    def spread_rest(frame, taps):
        def one(z, carry):
            for y in range(1, height + 1):
                spread(frame, taps, z, y, 0, 0, middle)
                spread(frame, taps, z, y, 2, middle, middle)
            for y, c in itertools.product((0, height + 1), range(3)):
                spread(frame, taps, z, y, c, 0, width)
            return carry

        lax.fori_loop(1, depth + 1, one, 0)

        def outer(i, carry):
            for y, c in itertools.product(range(height + 2), range(3)):
                spread(frame, taps, i * (depth + 1), y, c, 0, width)
            return carry

        lax.fori_loop(0, 2, outer, 0)

    def pair_conv(taps, matrix, z):
        total = None
        for a in range(3):
            rows = jnp.concatenate(
                [
                    taps[pl.ds(z + a, 2), pl.ds(r // 2, half_height), r % 2].reshape(
                        2 * half_height * width, 3 * skip
                    )
                    for r in range(4)
                ],
                axis=-1,
            )
            term = jnp.dot(
                rows,
                matrix[a].reshape(12 * skip, 2 * skip),
                preferred_element_type=jnp.float32,
            )
            total = term if total is None else total + term
        return total

    v_copies = send_planes(0, v_cells, volume, 0, depth, height)
    own_load.wait()

    def widen(z, carry):
        for y in range(1, height + 1):
            v_frame[z * slab + y, lead : lead + width, :] = v_cells[z, y].astype(jnp.float32)
        return carry

    lax.fori_loop(1, depth + 1, widen, 0)

    def begin_edges(slot, frame, n):
        take_edges(frame, edge_out.at[n], line_out.at[n], depth, height, width)
        arriving = (edge_in.at[n], line_in.at[n], corner_in.at[n])
        copies = send_edges(
            slot, edge_out.at[n], line_out.at[n], *arriving, depth, height
        )
        return arriving, copies

    v_arriving, v_edges = begin_edges(0, v_frame, 0)
    bottom_load = load(w_bottom, bottom_matrix)
    skip_loads = load_pairs(w_decode, skip, skip_pairs)
    up_loads = [
        load(
            w_up.at[a, b, c],
            up_matrix.at[:, pl.ds(((a * 2 + b) * 2 + c) * skip, skip)],
        )
        for a, b, c in itertools.product((0, 1), repeat=3)
    ]
    raised_loads = load_pairs(w_decode, 0, raised_pairs)
    for pairs in (encode_pairs, skip_pairs, raised_pairs):
        for a in range(3):
            pairs[a, 0, :, :, skip : 2 * skip] = jnp.zeros((3, skip, skip), jnp.bfloat16)
            pairs[a, 3, :, :, 0:skip] = jnp.zeros((3, skip, skip), jnp.bfloat16)
    spread_own(v_frame, v_taps)
    arrive(v_copies)
    halo_to_frame(v_cells, v_frame, depth, height, width)
    arrive(v_edges)
    put_edges(v_frame, *v_arriving, depth, height, width)
    spread_rest(v_frame, v_taps)
    for copy in encode_loads:
        copy.wait()
    encode_bias = jnp.concatenate([b_encode[...], b_encode[...]], axis=-1)

    def encode(i, carry):
        z = 2 * i
        values = rounded(leaky_relu(pair_conv(v_taps, encode_pairs, z) + encode_bias))
        values = values.reshape(2, half_height, width, 2 * skip)
        for dz in range(2):
            for y in range(height):
                cells = values[dz, y // 2, :, (y % 2) * skip : (y % 2 + 1) * skip]
                e_cells[z + dz + 1, y + 1] = cells
                e_frame[(z + dz + 1) * slab + y + 1, lead : lead + width, :] = cells.astype(
                    jnp.float32
                )
        return carry

    lax.fori_loop(0, half_depth, encode, 0)

    def gather_down(z, carry):
        for y in range(half_height):
            for a, b, c in itertools.product((0, 1), repeat=3):
                tap = (a * 2 + b) * 2 + c
                down_rows[z, y, :, tap * skip : (tap + 1) * skip] = rounded(
                    e_frame[
                        (2 * z + a + 1) * slab + 2 * y + b + 1,
                        pl.ds(lead + c, half_width, stride=2),
                        :,
                    ]
                )
        return carry

    lax.fori_loop(0, half_depth, gather_down, 0)
    down_load.wait()
    low_cells = half_depth * half_height * half_width
    coarse = jnp.dot(
        down_rows[...].reshape(low_cells, 8 * skip),
        down_matrix[...].reshape(8 * skip, deep),
        preferred_element_type=jnp.float32,
    )
    coarse = rounded(leaky_relu(coarse + b_down[...]))
    coarse = coarse.reshape(half_depth, half_height, half_width, deep)
    c_cells[1 : 1 + half_depth, 1 : 1 + half_height] = coarse
    c_copies = send_planes(2, c_cells, c_cells, 1, half_depth, half_height)
    for z in range(half_depth):
        for y in range(half_height):
            for h in deep_parts:
                c_frame[
                    h, (z + 1) * low_slab + y + 1, lead : lead + half_width, :
                ] = coarse[z, y, :, h * skip : (h + 1) * skip].astype(jnp.float32)

    low = (half_depth, half_height, half_width)
    c_edges = []
    for h in deep_parts:
        take_edges(
            c_frame.at[h], c_edge_out.at[:, :, lanes(h)], c_line_out.at[:, :, :, lanes(h)], *low
        )
    c_edges = send_edges(
        2, c_edge_out, c_line_out, c_edge_in, c_line_in, c_corner_in, half_depth, half_height
    )
    e_copies = send_planes(1, e_cells, e_cells, 1, depth, height)
    e_arriving, e_edges = begin_edges(1, e_frame, 1)
    spread_own(e_frame, e_taps)

    def decode_skip(i, carry):
        partial[i] = pair_conv(e_taps, skip_pairs, 2 * i)
        return carry

    arrive(c_copies)
    for h in deep_parts:
        halo_to_frame(c_cells.at[:, :, :, lanes(h)], c_frame.at[h], *low)
    arrive(c_edges)
    for h in deep_parts:
        put_edges(
            c_frame.at[h],
            c_edge_in.at[:, :, lanes(h)],
            c_line_in.at[:, :, :, lanes(h)],
            c_corner_in.at[:, :, :, lanes(h)],
            *low,
        )
    for z in range(half_depth + 2):
        for y in range(half_height + 2):
            for c, h in itertools.product(range(3), deep_parts):
                first = c * deep + h * skip
                c_taps[z, y, :, first : first + skip] = rounded(
                    c_frame[
                        h, z * low_slab + y, lead - 1 + c : lead - 1 + c + half_width, :
                    ]
                )
    bottom_load.wait()
    total = jnp.zeros((low_cells, deep), jnp.float32)
    for a in range(3):
        for b in range(3):
            total += jnp.dot(
                c_taps[a : a + half_depth, b : b + half_height].reshape(low_cells, 3 * deep),
                bottom_matrix[a, b].reshape(3 * deep, deep),
                preferred_element_type=jnp.float32,
            )
    bottom = rounded(leaky_relu(total + b_bottom[...]))
    for copy in up_loads:
        copy.wait()
    up_bias = jnp.concatenate([b_up[...], b_up[...]], axis=-1)
    for a in range(2):
        for b in range(2):
            first = (a * 2 + b) * 2 * skip
            lifted = jnp.dot(
                bottom, up_matrix[:, first : first + 2 * skip], preferred_element_type=jnp.float32
            )
            lifted = rounded(lifted + up_bias).astype(jnp.float32)
            lifted = lifted.reshape(half_depth, half_height, half_width, 2 * skip)
            for z in range(half_depth):
                for y in range(half_height):
                    plane = (2 * z + a + 1) * slab + 2 * y + b + 1
                    for c in range(2):
                        r_frame[plane, pl.ds(lead + c, half_width, stride=2), :] = lifted[
                            z, y, :, c * skip : (c + 1) * skip
                        ]

    def narrow_raised(z, carry):
        for y in range(height):
            r_cells[z + 1, y + 1] = rounded(
                r_frame[(z + 1) * slab + y + 1, lead : lead + width, :]
            )
        return carry

    lax.fori_loop(0, depth, narrow_raised, 0)
    r_copies = send_planes(3, r_cells, r_cells, 1, depth, height)

    r_arriving, r_edges = begin_edges(3, r_frame, 2)
    spread_own(r_frame, r_taps)
    arrive(e_copies)
    halo_to_frame(e_cells, e_frame, depth, height, width)
    arrive(e_edges)
    put_edges(e_frame, *e_arriving, depth, height, width)
    spread_rest(e_frame, e_taps)
    for copy in skip_loads:
        copy.wait()
    lax.fori_loop(0, half_depth, decode_skip, 0)
    arrive(r_copies)
    halo_to_frame(r_cells, r_frame, depth, height, width)
    arrive(r_edges)
    put_edges(r_frame, *r_arriving, depth, height, width)
    spread_rest(r_frame, r_taps)
    for copy in raised_loads:
        copy.wait()
    decode_bias = jnp.concatenate([b_decode[...], b_decode[...]], axis=-1)

    def decode(i, carry):
        values = pair_conv(r_taps, raised_pairs, 2 * i) + partial[i]
        values = (values + decode_bias).reshape(2, half_height, width, 2 * skip)
        for dz in range(2):
            for y in range(height):
                decoded[2 * i + dz, y] = values[dz, y // 2, :, (y % 2) * skip : (y % 2 + 1) * skip]
        return carry

    lax.fori_loop(0, half_depth, decode, 0)
    for going, copy in started:
        pl.when(going)(copy.wait_send)


def body(
    sizes,
    volume,
    w_encode,
    b_encode,
    w_down,
    b_down,
    w_bottom,
    b_bottom,
    w_up,
    b_up,
    w_decode,
    b_decode,
):
    depth, height, width, skip = volume.shape
    deep = w_down.shape[-1]
    half_depth, half_height, half_width = depth // 2, height // 2, width // 2
    planes, low_planes = depth + 2, half_depth + 2
    slab, low_slab = whole_tiles(height + 2), whole_tiles(half_height + 2)
    line, low_line = whole_tiles(planes), whole_tiles(low_planes)
    half = jnp.bfloat16
    cells = pltpu.VMEM((depth + 2, height + 2, width, skip), half)
    frame = pltpu.VMEM((line * slab, width + 2 * lead, skip), jnp.float32)
    taps = pltpu.VMEM((depth + 2, height // 2 + 1, 2, width, 3 * skip), half)
    pairs = pltpu.VMEM((3, 4, 3, skip, 2 * skip), half)
    far = pl.BlockSpec(memory_space=pltpu.HBM)
    bias = lambda size: pltpu.VMEM((1, size), jnp.float32)
    operands = (volume, w_encode, w_down, w_bottom, w_up, w_decode)
    operands += tuple(b.reshape(1, -1) for b in (b_encode, b_down, b_bottom, b_up, b_decode))
    total = pl.pallas_call(
        functools.partial(kernel, sizes),
        out_shape=jax.ShapeDtypeStruct(volume.shape, jnp.float32),
        in_specs=[far] * 11,
        out_specs=pl.BlockSpec(memory_space=pltpu.VMEM),
        scratch_shapes=[
            cells,
            cells,
            cells,
            pltpu.VMEM((half_depth + 2, half_height + 2, half_width, deep), half),
            frame,
            frame,
            frame,
            pltpu.VMEM((deep // skip, low_line * low_slab, half_width + 2 * lead, skip), jnp.float32),
            taps,
            taps,
            taps,
            pltpu.VMEM((half_depth + 2, half_height + 2, half_width, 3 * deep), half),
            pltpu.VMEM((3, 2, planes * slab, skip), half),
            pltpu.VMEM((3, 2, planes * slab, skip), half),
            pltpu.VMEM((3, 2, 2, line, skip), half),
            pltpu.VMEM((3, 2, 2, line, skip), half),
            pltpu.VMEM((3, 2, 4, slab, skip), half),
            pltpu.VMEM((2, low_planes * low_slab, deep), half),
            pltpu.VMEM((2, low_planes * low_slab, deep), half),
            pltpu.VMEM((2, 2, low_line, deep), half),
            pltpu.VMEM((2, 2, low_line, deep), half),
            pltpu.VMEM((2, 4, low_slab, deep), half),
            pairs,
            pairs,
            pairs,
            pltpu.VMEM(w_down.shape, half),
            pltpu.VMEM(w_bottom.shape, half),
            pltpu.VMEM((deep, 8 * skip), half),
            pltpu.VMEM((half_depth, half_height, half_width, 8 * skip), half),
            pltpu.VMEM((half_depth, height * width, 2 * skip), jnp.float32),
            bias(skip),
            bias(deep),
            bias(deep),
            bias(skip),
            bias(skip),
            pltpu.SemaphoreType.DMA((4, 8)),
            pltpu.SemaphoreType.DMA((4, 8)),
            pltpu.SemaphoreType.DMA((4, 2, 9)),
            pltpu.SemaphoreType.DMA((4, 2, 9)),
            pltpu.SemaphoreType.DMA((34,)),
        ],
        compiler_params=pltpu.CompilerParams(
            collective_id=0, has_side_effects=True, vmem_limit_bytes=52 * 2**20
        ),
    )(
        *(pltpu.with_memory_space_constraint(x, pltpu.HBM) for x in operands)
    )
    return rounded(leaky_relu(total))


def solution(mesh):
    sizes = (mesh.shape["wide"], mesh.shape["narrow"], mesh.shape["pair"])
    placed = P(("groups", "wide"), "narrow", "pair", None)
    return jax.shard_map(
        functools.partial(body, sizes),
        mesh=mesh,
        in_specs=(placed,) + (P(),) * 10,
        out_specs=placed,
        check_vma=False,
    )
```

```python
import functools
import itertools

import jax
import jax.numpy as jnp
from jax import lax
from jax.experimental import pallas as pl
from jax.experimental.pallas import tpu as pltpu
from jax.sharding import PartitionSpec as P

leak_slope = 0.01
MESH = pl.DeviceIdType.MESH
lead = 8
corners = list(itertools.product((0, 1), repeat=2))
plane_steps = [s for s in itertools.product((-1, 0, 1), repeat=2) if s != (0, 0)]
width_steps = (-1, 1)


def leaky_relu(values):
    return jnp.maximum(values, leak_slope * values)


def rounded(values):
    return values.astype(jnp.bfloat16)


def whole_tiles(cells):
    return cells + -cells % 16


def source_span(step, cells, base):
    if step == 0:
        return pl.ds(base, cells)
    return pl.ds(base + (0 if step < 0 else cells - 1), 1)


def target_span(step, cells):
    if step == 0:
        return pl.ds(1, cells)
    return pl.ds(cells + 1 if step < 0 else 0, 1)


def kernel(
    sizes,
    volume,
    w_encode,
    w_down,
    w_bottom,
    w_up,
    w_decode,
    b_encode_far,
    b_down_far,
    b_bottom_far,
    b_up_far,
    b_decode_far,
    decoded,
    v_cells,
    e_cells,
    r_cells,
    c_cells,
    v_frame,
    e_frame,
    r_frame,
    c_frame,
    v_taps,
    e_taps,
    r_taps,
    c_taps,
    edge_out,
    edge_in,
    line_out,
    line_in,
    corner_in,
    c_edge_out,
    c_edge_in,
    c_line_out,
    c_line_in,
    c_corner_in,
    encode_pairs,
    skip_pairs,
    raised_pairs,
    down_matrix,
    bottom_matrix,
    up_matrix,
    down_rows,
    partial,
    b_encode,
    b_down,
    b_bottom,
    b_up,
    b_decode,
    send_sem,
    recv_sem,
    edge_send_sem,
    edge_recv_sem,
    load_sem,
):
    depth, height, width, skip = volume.shape
    half_depth, half_height, half_width = depth // 2, height // 2, width // 2
    deep = w_down.shape[-1]
    deep_size, high_size, wide_size = sizes
    at_deep, at_high, at_wide = (lax.axis_index(name) for name in ("wide", "narrow", "pair"))

    def inside(place, step, size):
        return jnp.logical_and(place + step >= 0, place + step < size)

    def exists(step):
        near = jnp.logical_and(
            inside(at_deep, step[0], deep_size), inside(at_high, step[1], high_size)
        )
        if step[2] is None:
            return near
        return jnp.logical_and(near, inside(at_wide, step[2], wide_size))

    def reverse(step):
        return tuple(None if offset is None else -offset for offset in step)

    def place(step):
        column = 1 - at_wide if step[2] is None else at_wide + step[2]
        return {"wide": at_deep + step[0], "narrow": at_high + step[1], "pair": column}

    plane_used = [
        s
        for s in plane_steps
        if (s[0] == 0 or deep_size > 1) and (s[1] == 0 or high_size > 1)
    ]
    if wide_size == 2:
        width_used = ((None, 1 - at_wide),)
    else:
        width_used = tuple(zip(width_steps, (0, 1))) if wide_size > 1 else ()
    all_used = [s + (0,) for s in plane_used]
    all_used += [s + (x,) for s in [(0, 0)] + plane_used for x, _ in width_used]

    loads = []

    def load(source, target):
        copy = pltpu.make_async_copy(source, target, load_sem.at[len(loads)])
        copy.start()
        loads.append(copy)
        return copy

    own_load = load(volume, v_cells.at[pl.ds(1, depth), pl.ds(1, height)])

    def load_pairs(weight, first, target):
        return [
            load(
                weight.at[a, :, :, pl.ds(first, skip), :],
                target.at[a, pl.ds(j, 3), :, :, pl.ds(j * skip, skip)],
            )
            for a in range(3)
            for j in range(2)
        ]

    encode_loads = load_pairs(w_encode, 0, encode_pairs)
    encode_loads += [
        load(b_encode_far, b_encode),
        load(b_down_far, b_down),
        load(b_bottom_far, b_bottom),
        load(b_up_far, b_up),
        load(b_decode_far, b_decode),
    ]
    down_load = load(w_down, down_matrix)

    def zero_halo(cells, planes, rows):
        blank = jnp.zeros(cells.shape[2:], cells.dtype)
        for z in range(planes + 2):
            for y in range(rows + 2):
                if z in (0, planes + 1) or y in (0, rows + 1):
                    cells[z, y] = blank

    for cells in (v_cells, e_cells, r_cells):
        zero_halo(cells, depth, height)
    zero_halo(c_cells, half_depth, half_height)
    for arriving in (edge_in, line_in, corner_in, c_edge_in, c_line_in, c_corner_in):
        arriving[...] = jnp.zeros_like(arriving)

    barrier = pltpu.get_barrier_semaphore()
    for step in all_used:

        @pl.when(exists(step))
        def _():
            pl.semaphore_signal(barrier, inc=1, device_id=place(step), device_id_type=MESH)

    pl.semaphore_wait(barrier, sum(exists(step).astype(jnp.int32) for step in all_used))

    started = []

    def send(step, source, target, sends, receives):
        copy = pltpu.make_async_remote_copy(
            src_ref=source,
            dst_ref=target,
            send_sem=sends,
            recv_sem=receives,
            device_id=place(step),
            device_id_type=MESH,
        )
        pl.when(exists(step))(copy.start)
        started.append((exists(step), copy))
        return exists(reverse(step)), copy

    def send_planes(slot, cells, source, base, planes, rows):
        return [
            send(
                step + (0,),
                source.at[source_span(step[0], planes, base), source_span(step[1], rows, base)],
                cells.at[target_span(step[0], planes), target_span(step[1], rows)],
                send_sem.at[slot, k],
                recv_sem.at[slot, k],
            )
            for k, step in enumerate(plane_used)
        ]

    def send_edges(slot, edges, lines, arriving, arriving_lines, arriving_corners, planes, rows):
        slab = whole_tiles(rows + 2)
        copies = []
        for n, step in enumerate([(0, 0)] + plane_used):
            for lane, (across, k) in enumerate(width_used):
                if step[0] == 0:
                    here = there = pl.ds(slab, planes * slab)
                else:
                    here = pl.ds((1 if step[0] < 0 else planes) * slab, slab)
                    there = pl.ds((planes + 1 if step[0] < 0 else 0) * slab, slab)
                side = 1 if step[1] < 0 else 0
                if step[1] == 0:
                    source, target = edges.at[k, here], arriving.at[k, there]
                elif step[0] == 0:
                    source, target = lines.at[k, 1 - side], arriving_lines.at[k, side]
                else:
                    corner = corners.index((1 if step[0] < 0 else 0, side))
                    source, target = edges.at[k, here], arriving_corners.at[k, corner]
                copies.append(
                    send(
                        step + (across,),
                        source,
                        target,
                        edge_send_sem.at[slot, lane, n],
                        edge_recv_sem.at[slot, lane, n],
                    )
                )
        return copies

    def arrive(copies):
        for coming, copy in copies:
            pl.when(coming)(copy.wait_recv)

    def take_edges(frame, edges, lines, planes, rows, cells):
        slab = whole_tiles(rows + 2)
        count, pitch, channels = frame.shape
        flat = frame.reshape(count * pitch, channels)
        for k, column in enumerate((lead, lead + cells - 1)):
            edges[k] = rounded(flat[pl.ds(column, (planes + 2) * slab, stride=pitch), :])
            for j, y in enumerate((1, rows)):
                lines[k, j] = rounded(
                    flat[pl.ds(y * pitch + column, count // slab, stride=slab * pitch), :]
                )

    def put_edges(frame, arriving, arriving_lines, arriving_corners, planes, rows, cells):
        slab = whole_tiles(rows + 2)
        count, pitch, channels = frame.shape
        flat = frame.reshape(count * pitch, channels)
        for k, column in enumerate((lead + cells, lead - 1)):
            flat[pl.ds(column, (planes + 2) * slab, stride=pitch), :] = arriving[k].astype(
                jnp.float32
            )
            for j, y in enumerate((0, rows + 1)):
                flat[
                    pl.ds(y * pitch + column, count // slab, stride=slab * pitch), :
                ] = arriving_lines[k, j].astype(jnp.float32)
            for n, (deep_side, high_side) in enumerate(corners):
                plane = deep_side * (planes + 1) * slab + high_side * (rows + 1)
                row = 1 if high_side else rows
                frame[plane, column : column + 1, :] = arriving_corners[k, n].astype(jnp.float32)[
                    row : row + 1
                ]

    def lanes(h):
        return pl.ds(h * skip, skip)

    def halo_to_frame(cells, frame, planes, rows, span):
        for z in range(planes + 2):
            for y in range(rows + 2):
                if z in (0, planes + 1) or y in (0, rows + 1):
                    frame[z * whole_tiles(rows + 2) + y, lead : lead + span, :] = cells[z, y].astype(
                        jnp.float32
                    )

    deep_parts = range(deep // skip)

    slab = whole_tiles(height + 2)
    low_slab = whole_tiles(half_height + 2)
    middle = width // 2

    def spread(frame, taps, z, y, c, first, cells):
        begin = lead - 1 + c + first
        taps[z, y // 2, y % 2, first : first + cells, c * skip : (c + 1) * skip] = rounded(
            frame[z * slab + y, begin : begin + cells, :]
        )

    def spread_own(frame, taps):
        def one(z, carry):
            for y in range(1, height + 1):
                spread(frame, taps, z, y, 0, middle, middle)
                spread(frame, taps, z, y, 1, 0, width)
                spread(frame, taps, z, y, 2, 0, middle)
            return carry

        lax.fori_loop(1, depth + 1, one, 0)

    def spread_rest(frame, taps):
        def one(z, carry):
            for y in range(1, height + 1):
                spread(frame, taps, z, y, 0, 0, middle)
                spread(frame, taps, z, y, 2, middle, middle)
            for y, c in itertools.product((0, height + 1), range(3)):
                spread(frame, taps, z, y, c, 0, width)
            return carry

        lax.fori_loop(1, depth + 1, one, 0)

        def outer(i, carry):
            for y, c in itertools.product(range(height + 2), range(3)):
                spread(frame, taps, i * (depth + 1), y, c, 0, width)
            return carry

        lax.fori_loop(0, 2, outer, 0)

    def pair_conv(taps, matrix, z):
        total = None
        for a in range(3):
            rows = jnp.concatenate(
                [
                    taps[z + a, pl.ds(r // 2, half_height), r % 2].reshape(
                        half_height * width, 3 * skip
                    )
                    for r in range(4)
                ],
                axis=-1,
            )
            term = jnp.dot(
                rows,
                matrix[a].reshape(12 * skip, 2 * skip),
                preferred_element_type=jnp.float32,
            )
            total = term if total is None else total + term
        return total

    v_copies = send_planes(0, v_cells, volume, 0, depth, height)
    own_load.wait()

    def widen(z, carry):
        for y in range(1, height + 1):
            v_frame[z * slab + y, lead : lead + width, :] = v_cells[z, y].astype(jnp.float32)
        return carry

    lax.fori_loop(1, depth + 1, widen, 0)

    def begin_edges(slot, frame, n):
        take_edges(frame, edge_out.at[n], line_out.at[n], depth, height, width)
        arriving = (edge_in.at[n], line_in.at[n], corner_in.at[n])
        copies = send_edges(
            slot, edge_out.at[n], line_out.at[n], *arriving, depth, height
        )
        return arriving, copies

    v_arriving, v_edges = begin_edges(0, v_frame, 0)
    bottom_load = load(w_bottom, bottom_matrix)
    skip_loads = load_pairs(w_decode, skip, skip_pairs)
    up_loads = [
        load(
            w_up.at[a, b, c],
            up_matrix.at[:, pl.ds(((a * 2 + b) * 2 + c) * skip, skip)],
        )
        for a, b, c in itertools.product((0, 1), repeat=3)
    ]
    raised_loads = load_pairs(w_decode, 0, raised_pairs)
    for pairs in (encode_pairs, skip_pairs, raised_pairs):
        for a in range(3):
            pairs[a, 0, :, :, skip : 2 * skip] = jnp.zeros((3, skip, skip), jnp.bfloat16)
            pairs[a, 3, :, :, 0:skip] = jnp.zeros((3, skip, skip), jnp.bfloat16)
    spread_own(v_frame, v_taps)
    arrive(v_copies)
    halo_to_frame(v_cells, v_frame, depth, height, width)
    arrive(v_edges)
    put_edges(v_frame, *v_arriving, depth, height, width)
    spread_rest(v_frame, v_taps)
    for copy in encode_loads:
        copy.wait()
    encode_bias = jnp.concatenate([b_encode[...], b_encode[...]], axis=-1)

    def encode(z, carry):
        values = rounded(leaky_relu(pair_conv(v_taps, encode_pairs, z) + encode_bias))
        values = values.reshape(half_height, width, 2 * skip)
        for y in range(height):
            cells = values[y // 2, :, (y % 2) * skip : (y % 2 + 1) * skip]
            e_cells[z + 1, y + 1] = cells
            e_frame[(z + 1) * slab + y + 1, lead : lead + width, :] = cells.astype(jnp.float32)
        return carry

    lax.fori_loop(0, depth, encode, 0)

    def gather_down(z, carry):
        for y in range(half_height):
            for a, b, c in itertools.product((0, 1), repeat=3):
                tap = (a * 2 + b) * 2 + c
                down_rows[z, y, :, tap * skip : (tap + 1) * skip] = rounded(
                    e_frame[
                        (2 * z + a + 1) * slab + 2 * y + b + 1,
                        pl.ds(lead + c, half_width, stride=2),
                        :,
                    ]
                )
        return carry

    lax.fori_loop(0, half_depth, gather_down, 0)
    down_load.wait()
    low_cells = half_depth * half_height * half_width
    coarse = jnp.dot(
        down_rows[...].reshape(low_cells, 8 * skip),
        down_matrix[...].reshape(8 * skip, deep),
        preferred_element_type=jnp.float32,
    )
    coarse = rounded(leaky_relu(coarse + b_down[...]))
    coarse = coarse.reshape(half_depth, half_height, half_width, deep)
    c_cells[1 : 1 + half_depth, 1 : 1 + half_height] = coarse
    c_copies = send_planes(2, c_cells, c_cells, 1, half_depth, half_height)
    for z in range(half_depth):
        for y in range(half_height):
            for h in deep_parts:
                c_frame[
                    h, (z + 1) * low_slab + y + 1, lead : lead + half_width, :
                ] = coarse[z, y, :, h * skip : (h + 1) * skip].astype(jnp.float32)

    low = (half_depth, half_height, half_width)
    c_edges = []
    for h in deep_parts:
        take_edges(
            c_frame.at[h], c_edge_out.at[:, :, lanes(h)], c_line_out.at[:, :, :, lanes(h)], *low
        )
    c_edges = send_edges(
        2, c_edge_out, c_line_out, c_edge_in, c_line_in, c_corner_in, half_depth, half_height
    )
    e_copies = send_planes(1, e_cells, e_cells, 1, depth, height)
    e_arriving, e_edges = begin_edges(1, e_frame, 1)
    spread_own(e_frame, e_taps)

    def decode_skip(i, carry):
        partial[i] = pair_conv(e_taps, skip_pairs, i)
        return carry

    arrive(c_copies)
    for h in deep_parts:
        halo_to_frame(c_cells.at[:, :, :, lanes(h)], c_frame.at[h], *low)
    arrive(c_edges)
    for h in deep_parts:
        put_edges(
            c_frame.at[h],
            c_edge_in.at[:, :, lanes(h)],
            c_line_in.at[:, :, :, lanes(h)],
            c_corner_in.at[:, :, :, lanes(h)],
            *low,
        )
    for z in range(half_depth + 2):
        for y in range(half_height + 2):
            for c, h in itertools.product(range(3), deep_parts):
                first = c * deep + h * skip
                c_taps[z, y, :, first : first + skip] = rounded(
                    c_frame[
                        h, z * low_slab + y, lead - 1 + c : lead - 1 + c + half_width, :
                    ]
                )
    bottom_load.wait()
    total = jnp.zeros((low_cells, deep), jnp.float32)
    for a in range(3):
        for b in range(3):
            total += jnp.dot(
                c_taps[a : a + half_depth, b : b + half_height].reshape(low_cells, 3 * deep),
                bottom_matrix[a, b].reshape(3 * deep, deep),
                preferred_element_type=jnp.float32,
            )
    bottom = rounded(leaky_relu(total + b_bottom[...]))
    for copy in up_loads:
        copy.wait()
    up_bias = jnp.concatenate([b_up[...], b_up[...]], axis=-1)
    for a in range(2):
        for b in range(2):
            first = (a * 2 + b) * 2 * skip
            lifted = jnp.dot(
                bottom, up_matrix[:, first : first + 2 * skip], preferred_element_type=jnp.float32
            )
            lifted = rounded(lifted + up_bias).astype(jnp.float32)
            lifted = lifted.reshape(half_depth, half_height, half_width, 2 * skip)
            for z in range(half_depth):
                for y in range(half_height):
                    plane = (2 * z + a + 1) * slab + 2 * y + b + 1
                    for c in range(2):
                        r_frame[plane, pl.ds(lead + c, half_width, stride=2), :] = lifted[
                            z, y, :, c * skip : (c + 1) * skip
                        ]

    def narrow_raised(z, carry):
        for y in range(height):
            r_cells[z + 1, y + 1] = rounded(
                r_frame[(z + 1) * slab + y + 1, lead : lead + width, :]
            )
        return carry

    lax.fori_loop(0, depth, narrow_raised, 0)
    r_copies = send_planes(3, r_cells, r_cells, 1, depth, height)

    r_arriving, r_edges = begin_edges(3, r_frame, 2)
    spread_own(r_frame, r_taps)
    arrive(e_copies)
    halo_to_frame(e_cells, e_frame, depth, height, width)
    arrive(e_edges)
    put_edges(e_frame, *e_arriving, depth, height, width)
    spread_rest(e_frame, e_taps)
    for copy in skip_loads:
        copy.wait()
    lax.fori_loop(0, depth, decode_skip, 0)
    arrive(r_copies)
    halo_to_frame(r_cells, r_frame, depth, height, width)
    arrive(r_edges)
    put_edges(r_frame, *r_arriving, depth, height, width)
    spread_rest(r_frame, r_taps)
    for copy in raised_loads:
        copy.wait()
    decode_bias = jnp.concatenate([b_decode[...], b_decode[...]], axis=-1)

    def decode(i, carry):
        values = pair_conv(r_taps, raised_pairs, i) + partial[i]
        values = (values + decode_bias).reshape(half_height, width, 2 * skip)
        for y in range(height):
            decoded[i, y] = values[y // 2, :, (y % 2) * skip : (y % 2 + 1) * skip]
        return carry

    lax.fori_loop(0, depth, decode, 0)
    for going, copy in started:
        pl.when(going)(copy.wait_send)


def body(
    sizes,
    volume,
    w_encode,
    b_encode,
    w_down,
    b_down,
    w_bottom,
    b_bottom,
    w_up,
    b_up,
    w_decode,
    b_decode,
):
    depth, height, width, skip = volume.shape
    deep = w_down.shape[-1]
    half_depth, half_height, half_width = depth // 2, height // 2, width // 2
    planes, low_planes = depth + 2, half_depth + 2
    slab, low_slab = whole_tiles(height + 2), whole_tiles(half_height + 2)
    line, low_line = whole_tiles(planes), whole_tiles(low_planes)
    half = jnp.bfloat16
    cells = pltpu.VMEM((depth + 2, height + 2, width, skip), half)
    frame = pltpu.VMEM((line * slab, width + 2 * lead, skip), jnp.float32)
    taps = pltpu.VMEM((depth + 2, height // 2 + 1, 2, width, 3 * skip), half)
    pairs = pltpu.VMEM((3, 4, 3, skip, 2 * skip), half)
    far = pl.BlockSpec(memory_space=pltpu.HBM)
    bias = lambda size: pltpu.VMEM((1, size), jnp.float32)
    operands = (volume, w_encode, w_down, w_bottom, w_up, w_decode)
    operands += tuple(b.reshape(1, -1) for b in (b_encode, b_down, b_bottom, b_up, b_decode))
    total = pl.pallas_call(
        functools.partial(kernel, sizes),
        out_shape=jax.ShapeDtypeStruct(volume.shape, jnp.float32),
        in_specs=[far] * 11,
        out_specs=pl.BlockSpec(memory_space=pltpu.VMEM),
        scratch_shapes=[
            cells,
            cells,
            cells,
            pltpu.VMEM((half_depth + 2, half_height + 2, half_width, deep), half),
            frame,
            frame,
            frame,
            pltpu.VMEM((deep // skip, low_line * low_slab, half_width + 2 * lead, skip), jnp.float32),
            taps,
            taps,
            taps,
            pltpu.VMEM((half_depth + 2, half_height + 2, half_width, 3 * deep), half),
            pltpu.VMEM((3, 2, planes * slab, skip), half),
            pltpu.VMEM((3, 2, planes * slab, skip), half),
            pltpu.VMEM((3, 2, 2, line, skip), half),
            pltpu.VMEM((3, 2, 2, line, skip), half),
            pltpu.VMEM((3, 2, 4, slab, skip), half),
            pltpu.VMEM((2, low_planes * low_slab, deep), half),
            pltpu.VMEM((2, low_planes * low_slab, deep), half),
            pltpu.VMEM((2, 2, low_line, deep), half),
            pltpu.VMEM((2, 2, low_line, deep), half),
            pltpu.VMEM((2, 4, low_slab, deep), half),
            pairs,
            pairs,
            pairs,
            pltpu.VMEM(w_down.shape, half),
            pltpu.VMEM(w_bottom.shape, half),
            pltpu.VMEM((deep, 8 * skip), half),
            pltpu.VMEM((half_depth, half_height, half_width, 8 * skip), half),
            pltpu.VMEM((depth, height * width // 2, 2 * skip), jnp.float32),
            bias(skip),
            bias(deep),
            bias(deep),
            bias(skip),
            bias(skip),
            pltpu.SemaphoreType.DMA((4, 8)),
            pltpu.SemaphoreType.DMA((4, 8)),
            pltpu.SemaphoreType.DMA((4, 2, 9)),
            pltpu.SemaphoreType.DMA((4, 2, 9)),
            pltpu.SemaphoreType.DMA((34,)),
        ],
        compiler_params=pltpu.CompilerParams(
            collective_id=0, has_side_effects=True, vmem_limit_bytes=52 * 2**20
        ),
    )(
        *(pltpu.with_memory_space_constraint(x, pltpu.HBM) for x in operands)
    )
    return rounded(leaky_relu(total))


def solution(mesh):
    sizes = (mesh.shape["wide"], mesh.shape["narrow"], mesh.shape["pair"])
    placed = P(("groups", "wide"), "narrow", "pair", None)
    return jax.shard_map(
        functools.partial(body, sizes),
        mesh=mesh,
        in_specs=(placed,) + (P(),) * 10,
        out_specs=placed,
        check_vma=False,
    )
```
